128 devices in a mesh: gx: 4 (over y), gy: 4 (over z_lo, core), gz: 8 (over z_hi, x).
Axes of the slice: x: 4, y: 4, z: 4 (z_hi: 2, z_lo: 2; z = z_hi * 2 + z_lo), core: 2. Of those that a mesh axis runs over, the one named last changes fastest.
Arguments:
- positions: float32 [3, 16384], P(None, ('gx', 'gy', 'gz')), may hold values from -8 to 8
- atom_features: float32 [16384, 128], P(('gx', 'gy', 'gz')), may hold values from -6 to 6
- send_face: int32 [128, 6, 32], P(('gx', 'gy', 'gz')), may hold values from 0 to 127
- send_edge: int32 [128, 12, 8], P(('gx', 'gy', 'gz')), may hold values from 0 to 127
- send_corner: int32 [128, 8, 2], P(('gx', 'gy', 'gz')), may hold values from 0 to 127
- centre: int32 [786432], P(('gx', 'gy', 'gz')), may hold values from 0 to 127
- other: int32 [786432], P(('gx', 'gy', 'gz')), may hold values from 0 to 431
- edge_count: int32 [128], P(('gx', 'gy', 'gz')), may hold values from 1536 to 6144, as said below
- w_proj_a: float32 [128, 128], replicated, may hold values from -0.5 to 0.5
- w_proj_b: float32 [128, 128], replicated, may hold values from -0.5 to 0.5
- w_radial: float32 [8, 128], replicated, may hold values from -2 to 2
- w_first: bfloat16 [128, 128], replicated, may hold values from -0.5 to 0.5
- w_env: bfloat16 [128, 128], replicated, may hold values from -0.5 to 0.5
- w_value: bfloat16 [128, 128], replicated, may hold values from -0.5 to 0.5
- w_second: bfloat16 [256, 128], replicated, may hold values from -0.375 to 0.375
- w_out: bfloat16 [128], replicated, may hold values from -0.5 to 0.5
Outputs:
- forces: float32 [3, 16384], P(None, ('gx', 'gy', 'gz'))
- atom_energy: float32 [16384], P(('gx', 'gy', 'gz'))
- feature_grad: float32 [16384, 128], P(('gx', 'gy', 'gz'))
The draws below stay inside these ranges and needn't reach their ends.
Inputs may be any that keep to these rules, and one draw needn't show every extreme that they name: `edge_count`: some domain has exactly 6144 live edges in every draw.
All inputs are finite; a program needn't handle non-finite values.
Results may differ from the reference program's by a relative error of at most 0.035.
Values sent between devices are 32-bit elements; how exact they have to be, the bound alone decides.
A program may use at most 192 MiB of HBM per device.

```python
import math
import jax
import jax.numpy as jnp
import numpy as np
from jax import lax

C = 128
NB = 8
A_DEV = 128
GHOST = 32
GHOST_EDGE = 8
GHOST_CORNER = 2
E_DEV = 6144
TABLE = 432
ATOMS = 16384
EDGES = 786432
N_GX = 4
N_GY = 4
N_GZ = 8


def draw_edge_count(key, part):
    key = jax.random.fold_in(key, 7)
    first_key, second_key = jax.random.split(key)
    domains = N_GX * N_GY * N_GZ
    counts = jax.random.randint(first_key, (domains,), E_DEV // 4, E_DEV + 1)
    fullest = jax.random.randint(second_key, (), 0, domains)
    return jnp.where(jnp.arange(domains) == fullest, E_DEV, counts).astype(jnp.int32)


def touch_ends(result, rng, least, high):
    place = [jax.random.randint(jax.random.fold_in(rng, axis), (), 0, length) for axis, length in enumerate(result.shape)]
    main_axis = result.shape.index(max(result.shape))
    neighbour = place[:main_axis] + [(place[main_axis] + 1) % result.shape[main_axis]] + place[main_axis + 1:]
    return result.at[tuple(place)].set(least).at[tuple(neighbour)].set(high)


def block_levels(rng, dims, cuts, smallest, largest):
    def one(position, blocks):
        heights = jax.random.uniform(jax.random.fold_in(jax.random.fold_in(rng, 6), position), (blocks,), jnp.float32, smallest / len(cuts), largest / len(cuts))
        return jnp.repeat(jnp.exp(heights), dims[position] // blocks).reshape((-1,) + (1,) * (len(dims) - position - 1))

    loudness = one(*cuts[0])
    for cut in cuts[1:]:
        loudness = loudness * one(*cut)
    return loudness


def centred(own_key, extent, width, limit, cuts=(), held_as=jnp.bfloat16):
    result = width * jax.random.normal(own_key, extent, jnp.float32)
    if cuts:
        result = result * block_levels(own_key, extent, cuts, -0.22, 0.18)
    return jnp.clip(result, -limit, limit).astype(held_as)


def setup_inputs(seed: int = 0) -> dict:
    seeds = jax.random.split(jax.random.key(seed), 17)
    return {
        "positions": centred(seeds[0], (3, ATOMS), 1.5, 8.0, ((1, 128),), jnp.float32),
        "atom_features": centred(seeds[1], (ATOMS, C), 1.0, 6.0, ((0, 128),), jnp.float32),
        "send_face": touch_ends(jax.random.randint(seeds[2], (N_GX * N_GY * N_GZ, 6, GHOST), 0, A_DEV), jax.random.fold_in(seeds[2], 1), 0, A_DEV - 1).astype(jnp.int32),
        "send_edge": touch_ends(jax.random.randint(seeds[3], (N_GX * N_GY * N_GZ, 12, GHOST_EDGE), 0, A_DEV), jax.random.fold_in(seeds[3], 1), 0, A_DEV - 1).astype(jnp.int32),
        "send_corner": touch_ends(jax.random.randint(seeds[4], (N_GX * N_GY * N_GZ, 8, GHOST_CORNER), 0, A_DEV), jax.random.fold_in(seeds[4], 1), 0, A_DEV - 1).astype(jnp.int32),
        "centre": touch_ends(jax.random.randint(seeds[5], (EDGES,), 0, A_DEV), jax.random.fold_in(seeds[5], 1), 0, A_DEV - 1).astype(jnp.int32),
        "other": touch_ends(jax.random.randint(seeds[6], (EDGES,), 0, TABLE), jax.random.fold_in(seeds[6], 1), 0, TABLE - 1).astype(jnp.int32),
        "edge_count": draw_edge_count(jax.random.fold_in(seeds[16], 71), 0),
        "w_proj_a": centred(seeds[8], (C, C), C ** -0.5, 0.5, (), jnp.float32),
        "w_proj_b": centred(seeds[9], (C, C), C ** -0.5, 0.5, (), jnp.float32),
        "w_radial": centred(seeds[10], (NB, C), NB ** -0.5, 2.0, (), jnp.float32),
        "w_first": centred(seeds[11], (C, C), C ** -0.5, 0.5),
        "w_env": centred(seeds[12], (C, C), C ** -0.5, 0.5),
        "w_value": centred(seeds[13], (C, C), C ** -0.5, 0.5),
        "w_second": centred(seeds[14], (2 * C, C), (2 * C) ** -0.5, 0.375),
        "w_out": centred(seeds[15], (C,), C ** -0.5, 0.5),
    }


def offsets_table():
    rows = []
    for a in (-1, 0, 1):
        for b in (-1, 0, 1):
            for c in (-1, 0, 1):
                if a != 0 or b != 0 or c != 0:
                    rows.append((a, b, c))
    return np.array(rows, dtype=np.int32)

def class_keys():
    groups = [[], [], []]
    index = 0
    for a in (-1, 0, 1):
        for b in (-1, 0, 1):
            for c in (-1, 0, 1):
                if a != 0 or b != 0 or c != 0:
                    groups[abs(a) + abs(b) + abs(c) - 1].append(index)
                    index = index + 1
    return [np.array(group, dtype=np.int32) for group in groups]

def harmonics(unit):
    ux, uy, uz = (unit[0], unit[1], unit[2])
    return [jnp.ones_like(ux), ux, uy, uz, 1.732 * ux * uy, 1.732 * uy * uz, 1.732 * ux * uz, 0.866 * (ux * ux - uy * uy), 0.5 * (3.0 * uz * uz - 1.0)]

def local_energy(pos_tab, proj_a, proj_b, centre, other, valid, w_radial, w_first, w_env, w_value, w_second, w_out):
    n_own = proj_a.shape[0]
    disp = jnp.take(pos_tab, other, axis=1) - jnp.take(pos_tab, centre, axis=1)
    dist = jnp.sqrt(lax.optimization_barrier(jnp.sum(disp * disp, axis=0)) + 0.01)
    unit = disp / dist[None, :]
    envelope = 1.0 / (1.0 + (dist / 2.0) ** 2) ** 2
    orders = jnp.arange(1, w_radial.shape[0] + 1).astype(jnp.float32)
    basis = jnp.sin(orders[None, :] * (math.pi / 2.0) * dist[:, None]) / dist[:, None] * envelope[:, None]
    radial = jnp.dot(basis, w_radial, precision=lax.Precision.HIGHEST)
    mixed = (jnp.take(proj_a, centre, axis=0) + jnp.take(proj_b, other, axis=0) + radial).astype(jnp.bfloat16)
    first = jax.nn.silu(jnp.dot(mixed, w_first, preferred_element_type=jnp.float32)).astype(jnp.bfloat16)
    env_weight = jnp.dot(first, w_env, preferred_element_type=jnp.float32) * (envelope * valid)[:, None]
    value = jnp.dot(first, w_value, preferred_element_type=jnp.float32)
    total = jnp.zeros(value.shape, jnp.float32)
    for comp in harmonics(unit):
        env_m = jax.ops.segment_sum(env_weight * comp[:, None], centre, num_segments=n_own)
        total = total + comp[:, None] * jnp.take(env_m, centre, axis=0)
    scalar = (0.2 * value * total).astype(jnp.bfloat16)
    joined = jnp.concatenate([first, scalar], axis=1)
    second = jax.nn.silu(jnp.dot(joined, w_second, preferred_element_type=jnp.float32)).astype(jnp.bfloat16)
    edge_energy = jnp.dot(second, w_out, preferred_element_type=jnp.float32) * envelope * valid
    atom_energy = jax.ops.segment_sum(edge_energy, centre, num_segments=n_own)
    return (jnp.sum(edge_energy), atom_energy)

def reference(positions, atom_features, send_face, send_edge, send_corner, centre, other, edge_count, w_proj_a, w_proj_b, w_radial, w_first, w_env, w_value, w_second, w_out):
    n_dev = N_GX * N_GY * N_GZ
    high = lax.Precision.HIGHEST
    proj_a = jnp.dot(atom_features, w_proj_a, precision=high)
    proj_b = jnp.dot(atom_features, w_proj_b, precision=high)
    offs_np = offsets_table()
    dev = jnp.arange(n_dev).astype(jnp.int32)
    cx = dev // (N_GY * N_GZ)
    cy = dev // N_GZ % N_GY
    cz = dev % N_GZ
    own_idx = dev[:, None] * A_DEV + jnp.arange(A_DEV).astype(jnp.int32)[None, :]
    pieces = [own_idx]
    for keys, lists in zip(class_keys(), (send_face, send_edge, send_corner)):
        offs = jnp.asarray(offs_np[keys])
        src = ((cx[:, None] - offs[None, :, 0]) % N_GX * N_GY + (cy[:, None] - offs[None, :, 1]) % N_GY) * N_GZ + (cz[:, None] - offs[None, :, 2]) % N_GZ
        kidx = jnp.arange(keys.shape[0]).astype(jnp.int32)
        ghost_idx = src[:, :, None] * A_DEV + lists[src, kidx[None, :], :]
        pieces.append(ghost_idx.reshape(n_dev, -1))
    tables = jnp.concatenate(pieces, axis=1).astype(jnp.int32)

    def one(d):
        tab = tables[d]
        pos_tab = jnp.take(positions, tab, axis=1)
        pa = lax.dynamic_slice_in_dim(proj_a, (d * A_DEV).astype(jnp.int32), A_DEV, 0)
        pb = jnp.take(proj_b, tab, axis=0)
        ce = lax.dynamic_slice_in_dim(centre, (d * E_DEV).astype(jnp.int32), E_DEV, 0)
        ot = lax.dynamic_slice_in_dim(other, (d * E_DEV).astype(jnp.int32), E_DEV, 0)
        valid = (jnp.arange(E_DEV) < edge_count[d]).astype(jnp.float32)

        def energy(p, a, b):
            return local_energy(p, a, b, ce, ot, valid, w_radial, w_first, w_env, w_value, w_second, w_out)
        total, pullback, atom_e = jax.vjp(energy, pos_tab, pa, pb, has_aux=True)
        gp, ga, gb = pullback(jnp.ones((), jnp.float32))
        return (gp, ga, gb, atom_e)
    gp, ga, gb, atom_e = lax.map(one, dev)
    flat = tables.reshape(-1)
    grad_pos = jax.ops.segment_sum(jnp.transpose(gp, (0, 2, 1)).reshape(-1, 3), flat, num_segments=ATOMS)
    grad_b = jax.ops.segment_sum(gb.reshape(-1, gb.shape[2]), flat, num_segments=ATOMS)
    grad_a = ga.reshape(ATOMS, ga.shape[2])
    feature_grad = jnp.dot(grad_a, w_proj_a.T, precision=high) + jnp.dot(grad_b, w_proj_b.T, precision=high)
    return (-grad_pos.T, atom_e.reshape(ATOMS), feature_grad)
```

```python
import functools
import math
import jax
import jax.numpy as jnp
import numpy as np
from jax import lax
from jax.experimental import pallas as pl
from jax.experimental.pallas import tpu as pltpu
from jax.sharding import PartitionSpec as P

F32, BF16 = jnp.float32, jnp.bfloat16
NT = (((1,), (1,)), ((), ()))
NN = (((1,), (0,)), ((), ()))
TN = (((0,), (0,)), ((), ()))
TT = (((0,), (1,)), ((), ()))
ROWS = 608

def dot(a, b, dims=NN):
    return lax.dot_general(a, b, dims, preferred_element_type=F32)

def split(x, n):
    parts = []
    for _ in range(n):
        p = x.astype(BF16)
        parts.append(p)
        x = x - p.astype(F32)
    return parts

def sincos_turns(t):
    f = t - jnp.round(t)
    f2 = f * f
    s = f * _poly(f2, _SC)
    c = _poly(f2, _CC)
    return s, c

def _fit(fun, deg):
    x = np.cos(np.pi * (np.arange(400) + 0.5) / 400) * 0.125 + 0.125
    ch = np.polynomial.chebyshev.Chebyshev.fit(x, fun(x), deg, domain=[0, 0.25])
    return [float(v) for v in ch.convert(kind=np.polynomial.Polynomial).coef]

_SC = _fit(lambda y: np.sin(2 * np.pi * np.sqrt(y)) / np.sqrt(y), 7)
_CC = _fit(lambda y: np.cos(2 * np.pi * np.sqrt(y)), 7)

def _poly(x, cs):
    acc = cs[-1]
    for c in cs[-2::-1]:
        acc = acc * x + c
    return acc

def onehots(c, o, iota):
    cb = c.astype(F32).astype(BF16)
    far = jnp.maximum(o - 416, 0)
    o = jnp.where(o < 416, o, 416 + (far >> 1) * 8 + (far & 1))
    mask_c = iota == cb
    one, zero = jnp.ones((), BF16), jnp.zeros((), BF16)
    tiles = [jnp.where(mask_c, one, zero)]
    for t in range(4):
        ob = (o - 128 * t).astype(F32).astype(BF16)
        n = 128 if t < 3 else 96
        tiles.append(jnp.where(iota[:n] == ob, one, zero))
    return jnp.concatenate(tiles, axis=0)

def harm(ux, uy, uz):
    return [1.732 * ux * uy, 1.732 * uy * uz, 1.732 * ux * uz,
            0.866 * (ux * ux - uy * uy), 0.5 * (3.0 * uz * uz - 1.0)]

def weighted(mask, rows):
    zero = jnp.zeros((), BF16)
    return jnp.concatenate([jnp.where(mask, r.astype(BF16), zero) for r in rows], axis=0)

def assemble(env, scale):
    e = [env[:, 128 * m:128 * (m + 1)] * scale for m in range(9)]
    k = 1.732
    top = jnp.concatenate([e[0] - 0.5 * e[8], 0.5 * e[1], 0.5 * e[2], 0.5 * e[3]], axis=1)
    rx = jnp.concatenate([e[1], k * e[7], k * e[4], k * e[6]], axis=1)
    ry = jnp.concatenate([e[2], k * e[4], -k * e[7], k * e[5]], axis=1)
    rz = jnp.concatenate([e[3], k * e[6], k * e[5], 3.0 * e[8]], axis=1)
    return jnp.concatenate([top, rx, ry, rz], axis=0).astype(BF16)

def edge_kernel(eb, count_ref, centre_ref, other_ref, pos_ref, feat_ref, ghost_ref, pb_ref,
                wpa_ref, wr_ref, w1_ref, we_ref, wv_ref, w2_ref, wout_ref,
                grad_ref,
                first_s, slope_s, q_s, v_s, ds2_s, dv_s, rows_s, bp_s, tab_s, env_s, left_s, acc_s):
    E = centre_ref.shape[1]
    n = E // eb
    high = lax.Precision.HIGHEST
    iota = lax.broadcasted_iota(jnp.int32, (128, eb), 0).astype(F32).astype(BF16)
    pa = jnp.dot(feat_ref[...], wpa_ref[...], precision=high, preferred_element_type=F32)
    pos = pos_ref[...]
    own = pos
    ghost = ghost_ref[...]
    gpos = jnp.concatenate([ghost[:, 128:], jnp.zeros((32, 128), F32)], axis=0).T[:8, :352]
    top = jnp.concatenate([pa.T, pb_ref[...].T, jnp.concatenate([ghost[:, :128], jnp.zeros((32, 128), F32)], axis=0).T[:, :352]], axis=1)
    tab_s[0:128, :] = top.astype(BF16)
    low = jnp.concatenate([-own, own, gpos], axis=1)
    parts = split(low, 3)
    tab_s[128:160, :] = jnp.concatenate([p.astype(F32) for p in parts] + [jnp.zeros_like(low)], axis=0).astype(BF16)
    w1 = w1_ref[...]
    w1t = w1.astype(F32).T.astype(BF16)
    wevt = jnp.concatenate([we_ref[...].astype(F32).T, wv_ref[...].astype(F32).T], axis=0).astype(BF16)
    w2 = w2_ref[...]
    w2t = w2.astype(F32).T.astype(BF16)
    wback = jnp.concatenate([w2[:128], wv_ref[...], we_ref[...]], axis=1)
    w2b = w2[128:]
    wr = wr_ref[...]
    wr_hi = wr.astype(BF16).astype(F32)
    wr_lo = wr - wr_hi
    wrt = jnp.concatenate([wr_hi, wr_lo, wr_hi, jnp.zeros_like(wr)], axis=0).T.astype(BF16)
    wr2 = jnp.concatenate([wr_hi, wr_lo], axis=0).astype(BF16)
    wout = jnp.broadcast_to(wout_ref[...].astype(F32), (128, 128))
    wout = jnp.concatenate([wout] * (eb // 128), axis=1)
    count = count_ref[0]

    env_s[...] = jnp.zeros_like(env_s)

    def pass_a(i, _):
        ds = pl.ds(pl.multiple_of(i * eb, eb), eb)
        c, o = centre_ref[:, ds], other_ref[:, ds]
        oh = onehots(c, o, iota)
        p = dot(tab_s[...], oh)
        disp = p[128:136] + p[136:144] + p[144:152]
        dx, dy, dz = disp[0:1], disp[1:2], disp[2:3]
        sq = dx * dx + dy * dy + dz * dz + 0.01
        inv = lax.rsqrt(sq)
        dist = sq * inv
        ux, uy, uz = dx * inv, dy * inv, dz * inv
        s4 = 1.0 + 0.25 * dist * dist
        is4 = 1.0 / s4
        g = is4 * is4
        gd = -dist * g * is4
        lane = lax.broadcasted_iota(jnp.int32, (1, eb), 1) + i * eb
        valid = jnp.where(lane < count, 1.0, 0.0)
        gv = g * valid
        h = g * inv
        hd = (gd - h) * inv
        order = lax.broadcasted_iota(jnp.int32, (8, eb), 0).astype(F32) + 1.0
        sn, cs = sincos_turns(order * (0.25 * dist))
        basis = sn * h
        bp_s[:, ds] = order * (math.pi / 2) * cs * h + sn * hd
        rows_s[0:8, ds] = jnp.concatenate([ux, uy, uz, gv, inv, valid, gd, jnp.zeros_like(gd)], axis=0)
        b_hi = basis.astype(BF16).astype(F32)
        b4 = jnp.concatenate([b_hi, b_hi, basis - b_hi, jnp.zeros_like(basis)], axis=0).astype(BF16)
        mixed = (p[:128] + dot(wrt, b4)).astype(BF16)
        z1 = dot(w1t, mixed)
        sg = 0.5 * jnp.tanh(0.5 * z1) + 0.5
        f = z1 * sg
        first = f.astype(BF16)
        first_s[:, ds] = first
        slope_s[:, ds] = ((sg + f * (1.0 - sg)) * gv).astype(BF16)
        qv = dot(wevt, first).astype(BF16)
        q_s[:, ds] = qv[:128]
        v_s[:, ds] = qv[128:]
        g9 = weighted(iota == c.astype(F32).astype(BF16),
                      [gv, gv * ux, gv * uy, gv * uz] + [gv * y for y in harm(ux, uy, uz)])
        env_s[...] += dot(qv[:128], g9, NT)
        return 0
    lax.fori_loop(0, n, pass_a, 0)

    left_s[...] = assemble(env_s[...], 0.2)
    env_s[...] = jnp.zeros_like(env_s)

    def pass_b(i, _):
        ds = pl.ds(pl.multiple_of(i * eb, eb), eb)
        c = centre_ref[:, ds]
        rows = rows_s[:, ds]
        ux, uy, uz, gv = rows[0:1], rows[1:2], rows[2:3], rows[3:4]
        mask = iota == c.astype(F32).astype(BF16)
        m4 = weighted(mask, [jnp.ones_like(ux), ux, uy, uz])
        t4 = dot(left_s[...], m4)
        tx, ty, tz = t4[128:256], t4[256:384], t4[384:512]
        t = t4[:128] + (0.5 * ux) * tx + (0.5 * uy) * ty + (0.5 * uz) * tz
        v = v_s[:, ds].astype(F32)
        scal = (v * t).astype(BF16)
        z2 = dot(w2t, jnp.concatenate([first_s[:, ds], scal], axis=0))
        sg = 0.5 * jnp.tanh(0.5 * z2) + 0.5
        f = z2 * sg
        eo = jnp.sum(f.astype(BF16).astype(F32) * wout, axis=0, keepdims=True)
        ds2 = (wout * (sg + f * (1.0 - sg))).astype(BF16)
        ds2_s[:, ds] = ds2
        dsc = dot(w2b, ds2)
        dv_s[:, ds] = (t * dsc).astype(BF16)
        y = v * dsc
        du = [jnp.sum(y * k, axis=0, keepdims=True) for k in (tx, ty, tz)]
        rows_s[8:16, ds] = jnp.concatenate(du + [eo] + [jnp.zeros((4, eb), F32)], axis=0)
        g9 = jnp.concatenate([m4, weighted(mask, harm(ux, uy, uz))], axis=0)
        env_s[...] += dot((y * gv).astype(BF16), g9, NT)
        return 0
    lax.fori_loop(0, n, pass_b, 0)

    left_s[...] = assemble(env_s[...], 0.2)
    acc_s[...] = jnp.zeros_like(acc_s)

    def pass_c(i, _):
        ds = pl.ds(pl.multiple_of(i * eb, eb), eb)
        c, o = centre_ref[:, ds], other_ref[:, ds]
        rows = rows_s[:, ds]
        ux, uy, uz, gv = rows[0:1], rows[1:2], rows[2:3], rows[3:4]
        inv, valid, gd = rows[4:5], rows[5:6], rows[6:7]
        oh = onehots(c, o, iota)
        mask = iota == c.astype(F32).astype(BF16)
        m4 = weighted(mask, [jnp.ones_like(ux), ux, uy, uz])
        d4 = dot(left_s[...], m4)
        kx, ky, kz = d4[128:256], d4[256:384], d4[384:512]
        d = d4[:128] + (0.5 * ux) * kx + (0.5 * uy) * ky + (0.5 * uz) * kz
        q = q_s[:, ds].astype(F32)
        du = [jnp.sum(q * k, axis=0, keepdims=True) for k in (kx, ky, kz)]
        dgq = jnp.sum(q * d, axis=0, keepdims=True)
        df = dot(wback, jnp.concatenate([ds2_s[:, ds], dv_s[:, ds], d.astype(BF16)], axis=0))
        dz = (df * slope_s[:, ds].astype(F32)).astype(BF16)
        dm = dot(w1, dz).astype(BF16)
        db = dot(wr2, dm)
        db = db[:8] + db[8:]
        eo = rows[11:12]
        dux, duy, duz = [gv * (du[k] + rows[8 + k:9 + k]) for k in range(3)]
        dd = jnp.sum(db * bp_s[:, ds], axis=0, keepdims=True) + valid * (eo + dgq) * gd
        dd = dd - (dux * ux + duy * uy + duz * uz) * inv
        ee = eo * gv
        tail = jnp.concatenate([dux * inv + dd * ux, duy * inv + dd * uy, duz * inv + dd * uz, ee,
                                jnp.zeros((4, eb), F32)], axis=0)
        t_hi = tail.astype(BF16).astype(F32)
        low = jnp.concatenate([t_hi, tail - t_hi], axis=0).astype(BF16)
        acc_s[...] += dot(oh, jnp.concatenate([dm, low], axis=0), NT)
        return 0
    lax.fori_loop(0, n, pass_c, 0)
    acc = acc_s[...]
    low = acc[:, 128:136] + acc[:, 136:144]
    grad_ref[:, 0:128] = acc[:, :128]
    grad_ref[:, 128:256] = jnp.concatenate([low, jnp.zeros((ROWS, 120), F32)], axis=1)

def edge_call(count, centre, other, pos, feat, ghost, pb, wpa, wr, w1, we, wv, w2, wout, eb=3072):
    E = centre.shape[1]
    vm = pl.BlockSpec(memory_space=pltpu.VMEM)
    return pl.pallas_call(
        functools.partial(edge_kernel, eb),
        out_shape=jax.ShapeDtypeStruct((ROWS, 256), F32),
        in_specs=[pl.BlockSpec(memory_space=pltpu.SMEM)] + [vm] * 13,
        out_specs=vm,
        scratch_shapes=[pltpu.VMEM((128, E), BF16)] * 6 + [
            pltpu.VMEM((16, E), F32), pltpu.VMEM((8, E), F32),
            pltpu.VMEM((160, ROWS), BF16), pltpu.VMEM((128, 1152), F32), pltpu.VMEM((512, 512), BF16),
            pltpu.VMEM((ROWS, 144), F32)],
        compiler_params=pltpu.CompilerParams(vmem_limit_bytes=56 * 2**20),
    )(count, centre, other, pos, feat, ghost, pb, wpa, wr, w1, we, wv, w2, wout)


MESH = pl.DeviceIdType.MESH
GHOSTS = 352


def offset_list():
    cells = [(a, b, c) for a in (-1, 0, 1) for b in (-1, 0, 1) for c in (-1, 0, 1) if a or b or c]
    return sorted(cells, key=lambda o: abs(o[0]) + abs(o[1]) + abs(o[2]))


def blocks():
    out, start = [], 0
    for o in offset_list():
        width = (32, 8, 8)[abs(o[0]) + abs(o[1]) + abs(o[2]) - 1]
        out.append((o, start, width))
        start += width
    return out


def partner(offset, sign, sizes):
    at = [lax.axis_index(a) for a in ("gx", "gy", "gz")]
    return tuple(lax.rem(i + sign * o + n, n) for i, o, n in zip(at, offset, sizes))


def greet(sizes):
    barrier = pltpu.get_barrier_semaphore()
    for o in offset_list():
        pl.semaphore_signal(barrier, inc=1, device_id=partner(o, 1, sizes), device_id_type=MESH)
    pl.semaphore_wait(barrier, 26)


def exchange(src, base, dst, send, recv, sign, sizes):
    copies = []
    for k, (o, start, width) in enumerate(blocks()):
        copies.append(
            pltpu.make_async_remote_copy(
                src_ref=src.at[pl.ds(base + start, width)],
                dst_ref=dst.at[pl.ds(start, width)],
                send_sem=send.at[k],
                recv_sem=recv.at[k],
                device_id=partner(o, sign, sizes),
                device_id_type=MESH,
            )
        )
    for copy in copies:
        copy.start()
    return copies


def ghost_kernel(sizes, idx_ref, pos_ref, feat_ref, wpb_ref, ghost_ref, pb_ref, pos8_ref, out_s, in_s, send, recv):
    barrier = pltpu.get_barrier_semaphore()
    for o in offset_list():
        pl.semaphore_signal(barrier, inc=1, device_id=partner(o, 1, sizes), device_id_type=MESH)
    pb = jnp.dot(feat_ref[...], wpb_ref[...], precision=lax.Precision.HIGHEST, preferred_element_type=F32)
    pb_ref[...] = pb
    pos = jnp.concatenate([pos_ref[...], jnp.zeros((5, 128), F32)], axis=0)
    pos8_ref[...] = pos
    pick = (lax.broadcasted_iota(jnp.int32, (128, GHOSTS), 0) == idx_ref[...]).astype(F32).astype(BF16)
    out_s[:, 0:128] = dot(pick, pb.astype(BF16), TN)
    parts = jnp.concatenate([p.astype(F32) for p in split(pos, 3)], axis=0).astype(BF16)
    low = dot(parts, pick)
    low = low[0:8] + low[8:16] + low[16:24]
    low = jnp.concatenate([low, jnp.zeros((120, GHOSTS), F32)], axis=0)
    low = jnp.concatenate([low, jnp.zeros((128, 384 - GHOSTS), F32)], axis=1)
    out_s[:, 128:256] = low.T[:GHOSTS]
    pl.semaphore_wait(barrier, 26)
    copies = exchange(out_s, 0, in_s, send, recv, 1, sizes)
    for copy in copies:
        copy.wait()
    ghost_ref[...] = in_s[...]


def return_kernel(sizes, grad_ref, idx_ref, wpa_ref, wpb_ref, force_ref, energy_ref, fgrad_ref, in_s, send, recv):
    high = lax.Precision.HIGHEST
    greet(sizes)
    copies = exchange(grad_ref, 256, in_s, send, recv, -1, sizes)
    pick = (lax.broadcasted_iota(jnp.int32, (128, GHOSTS), 0) == idx_ref[...]).astype(F32)
    for copy in copies:
        copy.wait()
    own = grad_ref[128:256, :] + jnp.dot(pick, in_s[...], precision=high, preferred_element_type=F32)
    mid = grad_ref[0:128, :]
    fgrad_ref[...] = lax.dot_general(mid[:, :128], wpa_ref[...], NT, precision=high, preferred_element_type=F32) + lax.dot_general(
        own[:, :128], wpb_ref[...], NT, precision=high, preferred_element_type=F32
    )
    mid_t, own_t = mid[:, 128:].T, own[:, 128:].T
    force_ref[...] = mid_t[0:3] - own_t[0:3]
    energy_ref[...] = mid_t[3:4]


def local(
    sizes,
    positions,
    atom_features,
    send_face,
    send_edge,
    send_corner,
    centre,
    other,
    edge_count,
    w_proj_a,
    w_proj_b,
    w_radial,
    w_first,
    w_env,
    w_value,
    w_second,
    w_out,
):
    vm = pl.BlockSpec(memory_space=pltpu.VMEM)
    sems = [pltpu.SemaphoreType.DMA((26,)), pltpu.SemaphoreType.DMA((26,))]
    corner = jnp.pad(send_corner[0], ((0, 0), (0, 6)), constant_values=-1)
    idx = jnp.concatenate([send_face[0].reshape(-1), send_edge[0].reshape(-1), corner.reshape(-1)]).reshape(1, GHOSTS)
    ghost, pb, pos8 = pl.pallas_call(
        functools.partial(ghost_kernel, sizes),
        out_shape=[
            jax.ShapeDtypeStruct((GHOSTS, 256), F32),
            jax.ShapeDtypeStruct((128, 128), F32),
            jax.ShapeDtypeStruct((8, 128), F32),
        ],
        in_specs=[vm] * 4,
        out_specs=[vm] * 3,
        scratch_shapes=[pltpu.VMEM((GHOSTS, 256), F32), pltpu.VMEM((GHOSTS, 256), F32)] + sems,
        compiler_params=pltpu.CompilerParams(collective_id=0, has_side_effects=True),
    )(idx, positions, atom_features, w_proj_b)
    grad = edge_call(
        edge_count,
        centre.reshape(1, -1),
        other.reshape(1, -1),
        pos8,
        atom_features,
        ghost,
        pb,
        w_proj_a,
        w_radial,
        w_first,
        w_env,
        w_value,
        w_second,
        w_out.reshape(-1, 1),
    )
    force, energy, fgrad = pl.pallas_call(
        functools.partial(return_kernel, sizes),
        out_shape=[
            jax.ShapeDtypeStruct((3, 128), F32),
            jax.ShapeDtypeStruct((1, 128), F32),
            jax.ShapeDtypeStruct((128, 128), F32),
        ],
        in_specs=[vm] * 4,
        out_specs=[vm] * 3,
        scratch_shapes=[pltpu.VMEM((GHOSTS, 256), F32)] + sems,
        compiler_params=pltpu.CompilerParams(collective_id=1, has_side_effects=True),
    )(grad, idx, w_proj_a, w_proj_b)
    return force, energy.reshape(-1), fgrad


def solution(mesh):
    sizes = tuple(mesh.shape[a] for a in ("gx", "gy", "gz"))
    axes = ("gx", "gy", "gz")
    return jax.shard_map(
        functools.partial(local, sizes),
        mesh=mesh,
        in_specs=(
            P(None, axes),
            P(axes, None),
            P(axes, None, None),
            P(axes, None, None),
            P(axes, None, None),
            P(axes),
            P(axes),
            P(axes),
        )
        + (P(),) * 8,
        out_specs=(P(None, axes), P(axes), P(axes, None)),
        check_vma=False,
    )
```

```python
import functools
import math

import jax
import jax.numpy as jnp
import numpy as np
from jax import lax
from jax.experimental import pallas as pl
from jax.experimental.pallas import tpu as pltpu
from jax.sharding import PartitionSpec as P

F32, BF16 = jnp.float32, jnp.bfloat16
MESH = pl.DeviceIdType.MESH
NN = (((1,), (0,)), ((), ()))
NT = (((1,), (1,)), ((), ()))
TN = (((0,), (0,)), ((), ()))
OWN = 128
GHOSTS = 352
ROWS = 2 * OWN + GHOSTS


def dot(a, b, dims=NN):
    return lax.dot_general(a, b, dims, preferred_element_type=F32)


def split(x, n):
    parts = []
    for _ in range(n):
        part = x.astype(BF16)
        parts.append(part)
        x = x - part.astype(F32)
    return parts


def dot32(a, b, dims=NN):
    (ah, al), (bh, bl) = split(a, 2), split(b, 2)
    return dot(ah, bh, dims) + (dot(ah, bl, dims) + dot(al, bh, dims))


def fitted(fun, degree):
    x = np.cos(np.pi * (np.arange(400) + 0.5) / 400) * 0.125 + 0.125
    series = np.polynomial.chebyshev.Chebyshev.fit(x, fun(x), degree, domain=[0, 0.25])
    return [float(v) for v in series.convert(kind=np.polynomial.Polynomial).coef]


SINE = fitted(lambda y: np.sin(2 * np.pi * np.sqrt(y)) / np.sqrt(y), 7)
COSINE = fitted(lambda y: np.cos(2 * np.pi * np.sqrt(y)), 7)


def horner(x, coefs):
    acc = coefs[-1]
    for c in coefs[-2::-1]:
        acc = acc * x + c
    return acc


def sincos_turns(t):
    f = t - jnp.round(t)
    f2 = f * f
    return f * horner(f2, SINE), horner(f2, COSINE)


def select(mask, rows):
    zero = jnp.zeros((), BF16)
    return jnp.concatenate([jnp.where(mask, r.astype(BF16), zero) for r in rows], axis=0)


def moments(mask, gv, ux, uy, uz):
    gx, gy = gv * ux, gv * uy
    return select(mask, [gv, gx, gy, gv * uz, gx * uy, gx * ux - gy * uy])


def left_operand(s, scale):
    one, x, y, z, xy, xxyy = [s[:128, 128 * j : 128 * (j + 1)] * scale for j in range(6)]
    zx, zy, zz = [s[128:, 128 * j : 128 * (j + 1)] * scale for j in (1, 2, 3)]
    k = 1.732
    e4, e5, e6, e7, e8 = (k * k) * xy, (k * k) * zy, (k * k) * zx, (k * 0.866) * xxyy, 1.5 * zz - 0.5 * one
    return jnp.concatenate(
        [
            jnp.concatenate([one - 0.5 * e8, 0.5 * x, 0.5 * y, 0.5 * z], axis=1),
            jnp.concatenate([x, e7, e4, e6], axis=1),
            jnp.concatenate([y, e4, -e7, e5], axis=1),
            jnp.concatenate([z, e6, e5, 3.0 * e8], axis=1),
        ],
        axis=0,
    ).astype(BF16)


def offset_list():
    cells = [(a, b, c) for a in (-1, 0, 1) for b in (-1, 0, 1) for c in (-1, 0, 1) if a or b or c]
    return sorted(cells, key=lambda o: abs(o[0]) + abs(o[1]) + abs(o[2]))


def blocks():
    out, start = [], 0
    for o in offset_list():
        width = (32, 8, 8)[abs(o[0]) + abs(o[1]) + abs(o[2]) - 1]
        out.append((o, start, width))
        start += width
    return out


def partner(offset, sign, sizes):
    at = [lax.axis_index(a) for a in ("gx", "gy", "gz")]
    return tuple(lax.rem(i + sign * o + n, n) for i, o, n in zip(at, offset, sizes))


def greet(sizes):
    barrier = pltpu.get_barrier_semaphore()
    for o in offset_list():
        pl.semaphore_signal(barrier, inc=1, device_id=partner(o, 1, sizes), device_id_type=MESH)


def greeted():
    pl.semaphore_wait(pltpu.get_barrier_semaphore(), 26)


def exchange(src, dst, send, recv, sign, sizes):
    copies = []
    for k, (o, start, width) in enumerate(blocks()):
        copies.append(
            pltpu.make_async_remote_copy(
                src_ref=src.at[pl.ds(start, width)],
                dst_ref=dst.at[pl.ds(start, width)],
                send_sem=send.at[k],
                recv_sem=recv.at[k],
                device_id=partner(o, sign, sizes),
                device_id_type=MESH,
            )
        )
    for copy in reversed(copies):
        copy.start()
    return copies


def lanes_to_rows(x, rows):
    x = jnp.concatenate([x, jnp.zeros((120, x.shape[1]), F32)], axis=0)
    if x.shape[1] % 128:
        x = jnp.concatenate([x, jnp.zeros((128, -x.shape[1] % 128), F32)], axis=1)
    return x.T[:rows]


def rows_to_lanes(x):
    n = x.shape[0]
    if n % 128:
        x = jnp.concatenate([x, jnp.zeros((-n % 128, 128), F32)], axis=0)
    return x.T[:, :n]


def kernel(
    sizes,
    count_ref,
    pos_ref,
    feat_ref,
    face_ref,
    edge_ref,
    corner_ref,
    centre_ref,
    other_ref,
    wpa_ref,
    wpb_ref,
    wr_ref,
    w1_ref,
    we_ref,
    wv_ref,
    w2_ref,
    wout_ref,
    force_ref,
    energy_ref,
    fgrad_ref,
    out_s,
    in_s,
    ret_s,
    oh_s,
    p_s,
    first_s,
    slope_s,
    rows_s,
    bp_s,
    send_a,
    recv_a,
    send_b,
    recv_b,
):
    edges = centre_ref.shape[1]
    greet(sizes)

    feat = feat_ref[...]
    pb = dot32(feat, wpb_ref[...])
    pos = jnp.concatenate([pos_ref[...], jnp.zeros((5, 128), F32)], axis=0)
    face, edge, corner = face_ref[0], edge_ref[0], corner_ref[0]
    pad = jnp.full((1, 6), -1, jnp.int32)
    pieces = [face[k : k + 1] for k in range(6)] + [edge[k : k + 1] for k in range(12)]
    for k in range(8):
        pieces += [corner[k : k + 1], pad]
    slots = jnp.concatenate(pieces, axis=1)
    pick = (lax.broadcasted_iota(jnp.int32, (128, GHOSTS), 0) == slots).astype(F32).astype(BF16)
    out_s[:, 0:128] = dot(pick, pb.astype(BF16), TN)
    low = dot(jnp.concatenate([p.astype(F32) for p in split(pos, 3)], axis=0).astype(BF16), pick)
    out_s[:, 128:256] = lanes_to_rows(low[0:8] + low[8:16] + low[16:24], GHOSTS)
    greeted()
    ghosts = exchange(out_s, in_s, send_a, recv_a, 1, sizes)

    iota = lax.broadcasted_iota(jnp.int32, (128, edges), 0).astype(F32).astype(BF16)
    one, zero = jnp.ones((), BF16), jnp.zeros((), BF16)
    cb = centre_ref[...].astype(F32).astype(BF16)
    o = other_ref[...]
    far = jnp.maximum(o - 416, 0)
    o = jnp.where(o < 416, o, 416 + (far >> 1) * 8 + (far & 1))
    oh_s[0:128, :] = jnp.where(iota == cb, one, zero)
    for t in range(4):
        n = 128 if t < 3 else 96
        ob = (o - 128 * t).astype(F32).astype(BF16)
        oh_s[128 * (t + 1) : 128 * (t + 1) + n, :] = jnp.where(iota[:n] == ob, one, zero)
    pa = dot32(feat, wpa_ref[...])
    table = jnp.concatenate([pa.T, pb.T], axis=1).astype(BF16)
    both = jnp.concatenate([-pos, pos], axis=1)
    places = [p.astype(F32) for p in split(both, 3)]
    places = jnp.concatenate(places + [jnp.zeros_like(both)], axis=0).astype(BF16)
    p_s[...] = dot(jnp.concatenate([table, places], axis=0), oh_s[0:256, :])
    w1 = w1_ref[...]
    w1t = w1.astype(F32).T.astype(BF16)
    wevt = jnp.concatenate([we_ref[...].astype(F32).T, wv_ref[...].astype(F32).T], axis=0).astype(BF16)
    w2 = w2_ref[...]
    w2t = w2.astype(F32).T.astype(BF16)
    wback = jnp.concatenate([w2[:128], wv_ref[...], we_ref[...]], axis=1)
    w2b = w2[128:]
    wr = wr_ref[...]
    wr_hi = wr.astype(BF16).astype(F32)
    wr_lo = wr - wr_hi
    wrt = jnp.concatenate([wr_hi, wr_lo, wr_hi, jnp.zeros((104, 128), F32)], axis=0).T[:, :32].astype(BF16)
    wr2 = jnp.concatenate([wr_hi, wr_lo], axis=0).astype(BF16)
    wout = jnp.broadcast_to(wout_ref[...].astype(F32), (128, 128)).T
    wout = jnp.concatenate([wout] * (edges // 128), axis=1)
    count = count_ref[0]

    for copy in ghosts:
        copy.wait()
    got = in_s[...]
    gpos = rows_to_lanes(got[:, 128:])[:8]
    places = [p.astype(F32) for p in split(gpos, 3)]
    places = jnp.concatenate(places + [jnp.zeros_like(gpos)], axis=0).astype(BF16)
    table = jnp.concatenate([rows_to_lanes(got[:, :128]).astype(BF16), places], axis=0)

    p = p_s[...] + dot(table, oh_s[256:ROWS, :])
    disp = p[128:136] + p[136:144] + p[144:152]
    dx, dy, dz = disp[0:1], disp[1:2], disp[2:3]
    sq = dx * dx + dy * dy + dz * dz + 0.01
    inv = lax.rsqrt(sq)
    dist = sq * inv
    ux, uy, uz = dx * inv, dy * inv, dz * inv
    is4 = 1.0 / (1.0 + 0.25 * dist * dist)
    g = is4 * is4
    gd = -dist * g * is4
    lane = lax.broadcasted_iota(jnp.int32, (1, edges), 1)
    valid = jnp.where(lane < count, 1.0, 0.0)
    gv = g * valid
    h = g * inv
    hd = (gd - h) * inv
    order = lax.broadcasted_iota(jnp.int32, (8, edges), 0).astype(F32) + 1.0
    sn, cs = sincos_turns(order * (0.25 * dist))
    basis = sn * h
    bp_s[...] = order * (math.pi / 2) * cs * h + sn * hd
    rows_s[...] = jnp.concatenate([ux, uy, uz, gv, inv, valid, gd, jnp.zeros_like(gd)], axis=0)
    b_hi = basis.astype(BF16).astype(F32)
    b4 = jnp.concatenate([b_hi, b_hi, basis - b_hi, jnp.zeros_like(basis)], axis=0).astype(BF16)
    mixed = (p[:128] + dot(wrt, b4)).astype(BF16)
    z1 = dot(w1t, mixed)
    sg = 0.5 * jnp.tanh(0.5 * z1) + 0.5
    f = z1 * sg
    first = f.astype(BF16)
    first_s[...] = first
    slope_s[...] = ((sg + f * (1.0 - sg)) * gv).astype(BF16)
    qv = dot(wevt, first)
    q, v = qv[:128].astype(BF16), qv[128:].astype(BF16)
    mask = iota == cb
    env = dot(jnp.concatenate([q, (qv[:128] * uz).astype(BF16)], axis=0), moments(mask, gv, ux, uy, uz), NT)
    left = left_operand(env, 0.2)

    m4 = select(mask, [jnp.ones_like(ux), ux, uy, uz])
    t4 = dot(left, m4)
    tx, ty, tz = t4[128:256], t4[256:384], t4[384:512]
    t = t4[:128] + (0.5 * ux) * tx + (0.5 * uy) * ty + (0.5 * uz) * tz
    vf = v.astype(F32)
    z2 = dot(w2t, jnp.concatenate([first_s[...], (vf * t).astype(BF16)], axis=0))
    sg = 0.5 * jnp.tanh(0.5 * z2) + 0.5
    f = z2 * sg
    eo = jnp.sum(f.astype(BF16).astype(F32) * wout, axis=0, keepdims=True)
    ds2 = (wout * (sg + f * (1.0 - sg))).astype(BF16)
    dsc = dot(w2b, ds2)
    dv = (t * dsc).astype(BF16)
    y = vf * dsc
    du = [jnp.sum(y * k, axis=0, keepdims=True) for k in (tx, ty, tz)]
    env = dot(jnp.concatenate([y.astype(BF16), (y * uz).astype(BF16)], axis=0), moments(mask, gv, ux, uy, uz), NT)
    left = left_operand(env, 0.2)

    d4 = dot(left, m4)
    kx, ky, kz = d4[128:256], d4[256:384], d4[384:512]
    d = d4[:128] + (0.5 * ux) * kx + (0.5 * uy) * ky + (0.5 * uz) * kz
    qf = q.astype(F32)
    du = [a + jnp.sum(qf * k, axis=0, keepdims=True) for a, k in zip(du, (kx, ky, kz))]
    dgq = jnp.sum(qf * d, axis=0, keepdims=True)
    df = dot(wback, jnp.concatenate([ds2, dv, d.astype(BF16)], axis=0))
    dz1 = (df * slope_s[...].astype(F32)).astype(BF16)
    dm = dot(w1, dz1).astype(BF16)
    db = dot(wr2, dm)
    db = db[:8] + db[8:]
    rows = rows_s[...]
    ux, uy, uz, gv = rows[0:1], rows[1:2], rows[2:3], rows[3:4]
    inv, valid, gd = rows[4:5], rows[5:6], rows[6:7]
    dux, duy, duz = [gv * a for a in du]
    dd = jnp.sum(db * bp_s[...], axis=0, keepdims=True) + valid * (eo + dgq) * gd
    dd = dd - (dux * ux + duy * uy + duz * uz) * inv
    tail = [dux * inv + dd * ux, duy * inv + dd * uy, duz * inv + dd * uz, eo * gv, jnp.zeros((4, edges), F32)]
    tail = jnp.concatenate(tail, axis=0)
    tail_hi = tail.astype(BF16).astype(F32)
    final = jnp.concatenate([dm, jnp.concatenate([tail_hi, tail - tail_hi], axis=0).astype(BF16)], axis=0)

    acc = dot(oh_s[256:ROWS, :], final, NT)
    out_s[:, 0:128] = acc[:, :128]
    out_s[:, 128:256] = jnp.concatenate([acc[:, 128:136] + acc[:, 136:144], jnp.zeros((GHOSTS, 120), F32)], axis=1)
    returns = exchange(out_s, ret_s, send_b, recv_b, -1, sizes)
    acc = dot(oh_s[0:256, :], final, NT)
    low = acc[:, 128:136] + acc[:, 136:144]
    low = jnp.concatenate([low, jnp.zeros((256, 120), F32)], axis=1).T[:8]
    part = dot32(acc[:128, :128], wpa_ref[...], NT)
    own = acc[128:, :128]
    for copy in returns:
        copy.wait()
    got = ret_s[...]
    a_hi, a_lo = split(got[:, :128], 2)
    own = own + (dot(pick, a_hi) + dot(pick, a_lo))
    back = [dot(pick, x) for x in split(got[:, 128:], 3)]
    back = (back[0] + back[1] + back[2]).T[:8]
    fgrad_ref[...] = part + dot32(own, wpb_ref[...], NT)
    force_ref[...] = low[0:3, :128] - low[0:3, 128:] - back[0:3]
    energy_ref[...] = low[3:4, :128]


def local(
    sizes,
    positions,
    atom_features,
    send_face,
    send_edge,
    send_corner,
    centre,
    other,
    edge_count,
    w_proj_a,
    w_proj_b,
    w_radial,
    w_first,
    w_env,
    w_value,
    w_second,
    w_out,
):
    vm = pl.BlockSpec(memory_space=pltpu.VMEM)
    edges = centre.shape[0]
    force, energy, fgrad = pl.pallas_call(
        functools.partial(kernel, sizes),
        out_shape=[
            jax.ShapeDtypeStruct((3, 128), F32),
            jax.ShapeDtypeStruct((1, 128), F32),
            jax.ShapeDtypeStruct((128, 128), F32),
        ],
        in_specs=[pl.BlockSpec(memory_space=pltpu.SMEM)] + [vm] * 15,
        out_specs=[vm] * 3,
        scratch_shapes=[
            pltpu.VMEM((GHOSTS, 256), F32),
            pltpu.VMEM((GHOSTS, 256), F32),
            pltpu.VMEM((GHOSTS, 256), F32),
            pltpu.VMEM((ROWS, edges), BF16),
            pltpu.VMEM((160, edges), F32),
            pltpu.VMEM((128, edges), BF16),
            pltpu.VMEM((128, edges), BF16),
            pltpu.VMEM((8, edges), F32),
            pltpu.VMEM((8, edges), F32),
        ]
        + [pltpu.SemaphoreType.DMA((26,))] * 4,
        compiler_params=pltpu.CompilerParams(
            collective_id=0, has_side_effects=True, vmem_limit_bytes=60 * 2**20
        ),
    )(
        edge_count,
        positions,
        atom_features,
        send_face,
        send_edge,
        send_corner,
        centre.reshape(1, -1),
        other.reshape(1, -1),
        w_proj_a,
        w_proj_b,
        w_radial,
        w_first,
        w_env,
        w_value,
        w_second,
        w_out.reshape(1, -1),
    )
    return force, energy.reshape(-1), fgrad


def solution(mesh):
    axes = ("gx", "gy", "gz")
    sizes = tuple(mesh.shape[a] for a in axes)
    split_first = [P(axes, None), P(axes, None, None), P(axes, None, None), P(axes, None, None)]
    return jax.shard_map(
        functools.partial(local, sizes),
        mesh=mesh,
        in_specs=(P(None, axes), *split_first, P(axes), P(axes), P(axes)) + (P(),) * 8,
        out_specs=(P(None, axes), P(axes), P(axes, None)),
        check_vma=False,
    )
```

```python
import functools
import math

import jax
import jax.numpy as jnp
import numpy as np
from jax import lax
from jax.experimental import pallas as pl
from jax.experimental.pallas import tpu as pltpu
from jax.sharding import PartitionSpec as P

F32, BF16 = jnp.float32, jnp.bfloat16
MESH = pl.DeviceIdType.MESH
NN = (((1,), (0,)), ((), ()))
NT = (((1,), (1,)), ((), ()))
TN = (((0,), (0,)), ((), ()))
OWN = 128
GHOSTS = 352
ROWS = 2 * OWN + GHOSTS
WIDTH = 1024


def dot(a, b, dims=NN):
    return lax.dot_general(a, b, dims, preferred_element_type=F32)


def split(x, n):
    parts = []
    for _ in range(n):
        part = x.astype(BF16)
        parts.append(part)
        x = x - part.astype(F32)
    return parts


def dot32(a, b, dims=NN):
    (ah, al), (bh, bl) = split(a, 2), split(b, 2)
    return dot(ah, bh, dims) + (dot(ah, bl, dims) + dot(al, bh, dims))


def fitted(fun, degree):
    x = np.cos(np.pi * (np.arange(400) + 0.5) / 400) * 0.125 + 0.125
    series = np.polynomial.chebyshev.Chebyshev.fit(x, fun(x), degree, domain=[0, 0.25])
    return [float(v) for v in series.convert(kind=np.polynomial.Polynomial).coef]


SINE = fitted(lambda y: np.sin(2 * np.pi * np.sqrt(y)) / np.sqrt(y), 7)
COSINE = fitted(lambda y: np.cos(2 * np.pi * np.sqrt(y)), 7)


def horner(x, coefs):
    acc = coefs[-1]
    for c in coefs[-2::-1]:
        acc = acc * x + c
    return acc


def sincos_turns(t):
    f = t - jnp.round(t)
    f2 = f * f
    return f * horner(f2, SINE), horner(f2, COSINE)


def select(mask, rows):
    zero = jnp.zeros((), BF16)
    return jnp.concatenate([jnp.where(mask, r.astype(BF16), zero) for r in rows], axis=0)


def moments(mask, gv, ux, uy, uz):
    gx, gy = gv * ux, gv * uy
    return select(mask, [gv, gx, gy, gv * uz, gx * uy, gx * ux - gy * uy])


def left_operand(s, scale):
    one, x, y, z, xy, xxyy = [s[:128, 128 * j : 128 * (j + 1)] * scale for j in range(6)]
    zx, zy, zz = [s[128:, 128 * j : 128 * (j + 1)] * scale for j in (1, 2, 3)]
    k = 1.732
    e4, e5, e6, e7, e8 = (k * k) * xy, (k * k) * zy, (k * k) * zx, (k * 0.866) * xxyy, 1.5 * zz - 0.5 * one
    return jnp.concatenate(
        [
            jnp.concatenate([one - 0.5 * e8, 0.5 * x, 0.5 * y, 0.5 * z], axis=1),
            jnp.concatenate([x, e7, e4, e6], axis=1),
            jnp.concatenate([y, e4, -e7, e5], axis=1),
            jnp.concatenate([z, e6, e5, 3.0 * e8], axis=1),
        ],
        axis=0,
    ).astype(BF16)


def offset_list():
    cells = [(a, b, c) for a in (-1, 0, 1) for b in (-1, 0, 1) for c in (-1, 0, 1) if a or b or c]
    return sorted(cells, key=lambda o: abs(o[0]) + abs(o[1]) + abs(o[2]))


def blocks():
    out, start = [], 0
    for o in offset_list():
        width = (32, 8, 8)[abs(o[0]) + abs(o[1]) + abs(o[2]) - 1]
        out.append((o, start, width))
        start += width
    return out


def partner(offset, sign, sizes):
    at = [lax.axis_index(a) for a in ("gx", "gy", "gz")]
    return tuple(lax.rem(i + sign * o + n, n) for i, o, n in zip(at, offset, sizes))


def greet(sizes):
    barrier = pltpu.get_barrier_semaphore()
    for o in offset_list():
        pl.semaphore_signal(barrier, inc=1, device_id=partner(o, 1, sizes), device_id_type=MESH)


def greeted():
    pl.semaphore_wait(pltpu.get_barrier_semaphore(), 26)


def exchange(src, dst, send, recv, sign, sizes):
    copies = []
    for k, (o, start, width) in enumerate(blocks()):
        copies.append(
            pltpu.make_async_remote_copy(
                src_ref=src.at[pl.ds(start, width)],
                dst_ref=dst.at[pl.ds(start, width)],
                send_sem=send.at[k],
                recv_sem=recv.at[k],
                device_id=partner(o, sign, sizes),
                device_id_type=MESH,
            )
        )
    for copy in reversed(copies):
        copy.start()
    return copies


def lanes_to_rows(x, rows):
    x = jnp.concatenate([x, jnp.zeros((120, x.shape[1]), F32)], axis=0)
    if x.shape[1] % 128:
        x = jnp.concatenate([x, jnp.zeros((128, -x.shape[1] % 128), F32)], axis=1)
    return x.T[:rows]


def rows_to_lanes(x):
    n = x.shape[0]
    if n % 128:
        x = jnp.concatenate([x, jnp.zeros((-n % 128, 128), F32)], axis=0)
    return x.T[:, :n]


def staggered(make, count):
    live = []
    for k in range(count):
        live.append(make(k))
        live = [x for x in live if advance(x)]
    while live:
        live = [x for x in live if advance(x)]


def advance(x):
    try:
        next(x)
    except StopIteration:
        return False
    return True


def total(parts):
    return functools.reduce(jnp.add, parts)


def kernel(
    sizes,
    count_ref,
    pos_ref,
    feat_ref,
    face_ref,
    edge_ref,
    corner_ref,
    centre_ref,
    other_ref,
    wpa_ref,
    wpb_ref,
    wr_ref,
    w1_ref,
    we_ref,
    wv_ref,
    w2_ref,
    wout_ref,
    small_ref,
    fgrad_ref,
    out_s,
    in_s,
    ret_s,
    oh_s,
    p_s,
    first_s,
    slope_s,
    q_s,
    v_s,
    ds2_s,
    dv_s,
    final_s,
    saved_s,
    rows_s,
    bp_s,
    send_a,
    recv_a,
    send_b,
    recv_b,
):
    edges = centre_ref.shape[1]
    width = WIDTH
    greet(sizes)

    feat = feat_ref[...]
    w1 = w1_ref[...]
    w1b = sum(dot(x, w1) for x in split(wpb_ref[...], 3))
    pb = dot32(feat, w1b)
    pos = jnp.concatenate([pos_ref[...], jnp.zeros((5, 128), F32)], axis=0)
    edge = jnp.concatenate([edge_ref[0].astype(F32), jnp.zeros((8, 116), F32)], axis=1)
    corner = jnp.concatenate([corner_ref[0].astype(F32), jnp.full((6, 8), -1.0, F32)], axis=0)
    corner = jnp.concatenate([corner, jnp.zeros((8, 120), F32)], axis=1)
    lists = jnp.concatenate([edge, corner, jnp.zeros((112, 128), F32)], axis=0).T.astype(jnp.int32)
    pieces = [face_ref[k] for k in range(6)] + [lists[k : k + 1, 0:8] for k in range(12)]
    pieces += [lists[k : k + 1, 8:16] for k in range(8)]
    slots = jnp.concatenate(pieces, axis=1)
    pick = (lax.broadcasted_iota(jnp.int32, (128, GHOSTS), 0) == slots).astype(F32).astype(BF16)
    out_s[:, 0:128] = dot(pick, pb.astype(BF16), TN)
    low = dot(jnp.concatenate([p.astype(F32) for p in split(pos, 3)], axis=0).astype(BF16), pick)
    out_s[:, 128:256] = lanes_to_rows(low[0:8] + low[8:16] + low[16:24], GHOSTS)
    greeted()
    ghosts = exchange(out_s, in_s, send_a, recv_a, 1, sizes)

    iota = lax.broadcasted_iota(jnp.int32, (128, edges), 0).astype(F32).astype(BF16)
    one, zero = jnp.ones((), BF16), jnp.zeros((), BF16)
    cb = centre_ref[...].astype(F32).astype(BF16)
    o = other_ref[...]
    far = jnp.maximum(o - 416, 0)
    o = jnp.where(o < 416, o, 416 + (far >> 1) * 8 + (far & 1))
    oh_s[0:128, :] = jnp.where(iota == cb, one, zero)
    for t in range(4):
        n = 128 if t < 3 else 96
        ob = (o - 128 * t).astype(F32).astype(BF16)
        oh_s[128 * (t + 1) : 128 * (t + 1) + n, :] = jnp.where(iota[:n] == ob, one, zero)
    w1a = sum(dot(x, w1) for x in split(wpa_ref[...], 3))
    pa = dot32(feat, w1a)
    table = jnp.concatenate([pa.T, pb.T], axis=1).astype(BF16)
    both = jnp.concatenate([-pos, pos], axis=1)
    places = [p.astype(F32) for p in split(both, 3)]
    places = jnp.concatenate(places + [jnp.zeros_like(both)], axis=0).astype(BF16)
    p_s[...] = dot(jnp.concatenate([table, places], axis=0), oh_s[0:256, :])
    wevt = jnp.concatenate([we_ref[...].astype(F32).T, wv_ref[...].astype(F32).T], axis=0).astype(BF16)
    w2 = w2_ref[...]
    w2t = w2.astype(F32).T.astype(BF16)
    wback = jnp.concatenate([w2[:128], wv_ref[...], we_ref[...]], axis=1)
    w2b = w2[128:]
    wr = sum(dot(x, w1) for x in split(jnp.concatenate([wr_ref[...], jnp.zeros((8, 128), F32)], axis=0), 3))[:8]
    wr_hi = wr.astype(BF16).astype(F32)
    wr_lo = wr - wr_hi
    wrt = jnp.concatenate([wr_hi, wr_lo, wr_hi, jnp.zeros((104, 128), F32)], axis=0).T[:, :32].astype(BF16)
    wr2 = jnp.concatenate([wr_hi, wr_lo], axis=0).astype(BF16)
    wout = jnp.broadcast_to(wout_ref[...].astype(F32), (128, 128)).T
    wout = jnp.concatenate([wout] * (edges // 128), axis=1)
    count = count_ref[0]

    for copy in ghosts:
        copy.wait()
    got = in_s[...]
    gpos = rows_to_lanes(got[:, 128:])[:8]
    places = [p.astype(F32) for p in split(gpos, 3)]
    places = jnp.concatenate(places + [jnp.zeros_like(gpos)], axis=0).astype(BF16)
    table = jnp.concatenate([rows_to_lanes(got[:, :128]).astype(BF16), places], axis=0)

    def group(k):
        at = slice(k * width, (k + 1) * width)
        cols = pl.ds(k * width, width)

        p = p_s[:, cols] + dot(table, oh_s[256:ROWS, cols])
        yield
        disp = p[128:136] + p[136:144] + p[144:152]
        dx, dy, dz = disp[0:1], disp[1:2], disp[2:3]
        sq = dx * dx + dy * dy + dz * dz + 0.01
        inv = lax.rsqrt(sq)
        dist = sq * inv
        ux, uy, uz = dx * inv, dy * inv, dz * inv
        is4 = 1.0 / (1.0 + 0.25 * dist * dist)
        g = is4 * is4
        gd = -dist * g * is4
        lane = lax.broadcasted_iota(jnp.int32, (1, width), 1) + k * width
        valid = jnp.where(lane < count, 1.0, 0.0)
        gv = g * valid
        h = g * inv
        hd = (gd - h) * inv
        order = lax.broadcasted_iota(jnp.int32, (8, width), 0).astype(F32) + 1.0
        sn, cs = sincos_turns(order * (0.25 * dist))
        basis = sn * h
        bp_s[:, cols] = order * (math.pi / 2) * cs * h + sn * hd
        rows_s[:, cols] = jnp.concatenate([ux, uy, uz, gv, inv, valid, gd, jnp.zeros_like(gd)], axis=0)
        b_hi = basis.astype(BF16).astype(F32)
        b4 = jnp.concatenate([b_hi, b_hi, basis - b_hi, jnp.zeros_like(basis)], axis=0).astype(BF16)
        z1 = p[:128] + dot(wrt, b4)
        yield
        sg = 0.5 * jnp.tanh(0.5 * z1) + 0.5
        f = z1 * sg
        first = f.astype(BF16)
        first_s[:, cols] = first
        slope_s[:, cols] = ((sg + f * (1.0 - sg)) * gv).astype(BF16)
        qv = dot(wevt, first)
        yield
        q_s[:, cols] = qv[:128].astype(BF16)
        v_s[:, cols] = qv[128:].astype(BF16)
        mask = iota[:, at] == cb[:, at]
        pair = jnp.concatenate([qv[:128].astype(BF16), (qv[:128] * uz).astype(BF16)], axis=0)
        env.append(dot(pair, moments(mask, gv, ux, uy, uz), NT))

    def group_b(k):
        at = slice(k * width, (k + 1) * width)
        cols = pl.ds(k * width, width)
        rows = rows_s[:, cols]
        ux, uy, uz, gv = rows[0:1], rows[1:2], rows[2:3], rows[3:4]
        mask = iota[:, at] == cb[:, at]
        t4 = dot(left, select(mask, [jnp.ones_like(ux), ux, uy, uz]))
        yield
        tx, ty, tz = t4[128:256], t4[256:384], t4[384:512]
        t = t4[:128] + (0.5 * ux) * tx + (0.5 * uy) * ty + (0.5 * uz) * tz
        vf = v_s[:, cols].astype(F32)
        z2 = dot(w2t, jnp.concatenate([first_s[:, cols], (vf * t).astype(BF16)], axis=0))
        yield
        sg = 0.5 * jnp.tanh(0.5 * z2) + 0.5
        f = z2 * sg
        eo = jnp.sum(f.astype(BF16).astype(F32) * wout[:, at], axis=0, keepdims=True)
        ds2 = (wout[:, at] * (sg + f * (1.0 - sg))).astype(BF16)
        ds2_s[:, cols] = ds2
        dsc = dot(w2b, ds2)
        yield
        dv_s[:, cols] = (t * dsc).astype(BF16)
        y = vf * dsc
        du = [jnp.sum(y * c, axis=0, keepdims=True) for c in (tx, ty, tz)]
        saved_s[:, cols] = jnp.concatenate(du + [eo, jnp.zeros((4, width), F32)], axis=0)
        pair = jnp.concatenate([y.astype(BF16), (y * uz).astype(BF16)], axis=0)
        env.append(dot(pair, moments(mask, gv, ux, uy, uz), NT))

    def group_c(k):
        at = slice(k * width, (k + 1) * width)
        cols = pl.ds(k * width, width)
        rows = rows_s[:, cols]
        ux, uy, uz, gv = rows[0:1], rows[1:2], rows[2:3], rows[3:4]
        mask = iota[:, at] == cb[:, at]
        d4 = dot(left, select(mask, [jnp.ones_like(ux), ux, uy, uz]))
        yield
        kx, ky, kz = d4[128:256], d4[256:384], d4[384:512]
        d = d4[:128] + (0.5 * ux) * kx + (0.5 * uy) * ky + (0.5 * uz) * kz
        qf = q_s[:, cols].astype(F32)
        saved = saved_s[:, cols]
        dux, duy, duz = [saved[j : j + 1] + jnp.sum(qf * c, axis=0, keepdims=True) for j, c in enumerate((kx, ky, kz))]
        dgq = jnp.sum(qf * d, axis=0, keepdims=True)
        df = dot(wback, jnp.concatenate([ds2_s[:, cols], dv_s[:, cols], d.astype(BF16)], axis=0))
        yield
        dz1 = (df * slope_s[:, cols].astype(F32)).astype(BF16)
        db = dot(wr2, dz1)
        yield
        db = db[:8] + db[8:]
        inv, valid, gd = rows[4:5], rows[5:6], rows[6:7]
        dux, duy, duz = gv * dux, gv * duy, gv * duz
        eo = saved[3:4]
        dd = jnp.sum(db * bp_s[:, cols], axis=0, keepdims=True) + valid * (eo + dgq) * gd
        dd = dd - (dux * ux + duy * uy + duz * uz) * inv
        tail = [dux * inv + dd * ux, duy * inv + dd * uy, duz * inv + dd * uz, eo * gv, jnp.zeros((4, width), F32)]
        tail = jnp.concatenate(tail, axis=0)
        tail_hi = tail.astype(BF16).astype(F32)
        low = jnp.concatenate([tail_hi, tail - tail_hi], axis=0).astype(BF16)
        final = jnp.concatenate([dz1, low], axis=0)
        final_s[:, cols] = final
        env.append(dot(oh_s[256:ROWS, cols], final, NT))

    env = []
    staggered(group, edges // width)
    left = left_operand(total(env), 0.2)
    env = []
    staggered(group_b, edges // width)
    left = left_operand(total(env), 0.2)
    env = []
    staggered(group_c, edges // width)

    acc = total(env)
    out_s[:, 0:128] = acc[:, :128]
    out_s[:, 128:256] = jnp.concatenate([acc[:, 128:136] + acc[:, 136:144], jnp.zeros((GHOSTS, 120), F32)], axis=1)
    returns = exchange(out_s, ret_s, send_b, recv_b, -1, sizes)
    acc = dot(oh_s[0:256, :], final_s[...], NT)
    low = acc[:, 128:136] + acc[:, 136:144]
    low = jnp.concatenate([low, jnp.zeros((256, 120), F32)], axis=1).T[:8]
    part = dot32(acc[:128, :128], w1a, NT)
    own = acc[128:, :128]
    for copy in returns:
        copy.wait()
    got = ret_s[...]
    a_hi, a_lo = split(got[:, :128], 2)
    own = own + (dot(pick, a_hi) + dot(pick, a_lo))
    back = [dot(pick, x) for x in split(got[:, 128:], 3)]
    back = (back[0] + back[1] + back[2]).T[:8]
    fgrad_ref[...] = part + dot32(own, w1b, NT)
    small_ref[...] = jnp.concatenate([low[0:3, :128] - low[0:3, 128:] - back[0:3], low[3:8, :128]], axis=0)


def place(small_ref, wide_ref, force_ref, energy_ref, fgrad_ref):
    force_ref[...] = small_ref[0:3, :]
    energy_ref[...] = small_ref[3:4, :]
    fgrad_ref[...] = wide_ref[...]


def local(
    sizes,
    positions,
    atom_features,
    send_face,
    send_edge,
    send_corner,
    centre,
    other,
    edge_count,
    w_proj_a,
    w_proj_b,
    w_radial,
    w_first,
    w_env,
    w_value,
    w_second,
    w_out,
):
    vm = pl.BlockSpec(memory_space=pltpu.VMEM)
    edges = centre.shape[0]
    small, wide = pl.pallas_call(
        functools.partial(kernel, sizes),
        out_shape=[jax.ShapeDtypeStruct((8, 128), F32), jax.ShapeDtypeStruct((128, 128), F32)],
        in_specs=[pl.BlockSpec(memory_space=pltpu.SMEM)] + [vm] * 15,
        out_specs=[vm] * 2,
        scratch_shapes=[
            pltpu.VMEM((GHOSTS, 256), F32),
            pltpu.VMEM((GHOSTS, 256), F32),
            pltpu.VMEM((GHOSTS, 256), F32),
            pltpu.VMEM((ROWS, edges), BF16),
            pltpu.VMEM((160, edges), F32),
            *[pltpu.VMEM((128, edges), BF16)] * 6,
            pltpu.VMEM((144, edges), BF16),
            pltpu.VMEM((8, edges), F32),
            pltpu.VMEM((8, edges), F32),
            pltpu.VMEM((8, edges), F32),
        ]
        + [pltpu.SemaphoreType.DMA((26,))] * 4,
        compiler_params=pltpu.CompilerParams(
            collective_id=0, has_side_effects=True, vmem_limit_bytes=60 * 2**20
        ),
    )(
        edge_count,
        positions,
        atom_features,
        jnp.transpose(send_face, (1, 0, 2)),
        jnp.transpose(send_edge, (0, 2, 1)),
        jnp.transpose(send_corner, (0, 2, 1)),
        centre.reshape(1, -1),
        other.reshape(1, -1),
        w_proj_a,
        w_proj_b,
        w_radial,
        w_first,
        w_env,
        w_value,
        w_second,
        w_out.reshape(1, -1),
    )
    force, energy, fgrad = pl.pallas_call(
        place,
        out_shape=[
            jax.ShapeDtypeStruct((3, 128), F32),
            jax.ShapeDtypeStruct((1, 128), F32),
            jax.ShapeDtypeStruct((128, 128), F32),
        ],
        in_specs=[vm] * 2,
        out_specs=[vm] * 3,
    )(small, wide)
    return force, energy.reshape(-1), fgrad


def solution(mesh):
    axes = ("gx", "gy", "gz")
    sizes = tuple(mesh.shape[a] for a in axes)
    split_first = [P(axes, None), P(axes, None, None), P(axes, None, None), P(axes, None, None)]
    return jax.shard_map(
        functools.partial(local, sizes),
        mesh=mesh,
        in_specs=(P(None, axes), *split_first, P(axes), P(axes), P(axes)) + (P(),) * 8,
        out_specs=(P(None, axes), P(axes), P(axes, None)),
        check_vma=False,
    )
```

```python
import functools
import math

import jax
import jax.numpy as jnp
import numpy as np
from jax import lax
from jax.experimental import pallas as pl
from jax.experimental.pallas import tpu as pltpu
from jax.sharding import PartitionSpec as P

F32, BF16 = jnp.float32, jnp.bfloat16
MESH = pl.DeviceIdType.MESH
NN = (((1,), (0,)), ((), ()))
NT = (((1,), (1,)), ((), ()))
TN = (((0,), (0,)), ((), ()))
OWN = 128
GHOSTS = 352
ROWS = 2 * OWN + GHOSTS
WIDTH = 1024


def dot(a, b, dims=NN):
    return lax.dot_general(a, b, dims, preferred_element_type=F32)


def split(x, n):
    parts = []
    for _ in range(n):
        part = x.astype(BF16)
        parts.append(part)
        x = x - part.astype(F32)
    return parts


def dot32(a, b, dims=NN):
    (ah, al), (bh, bl) = split(a, 2), split(b, 2)
    return dot(ah, bh, dims) + (dot(ah, bl, dims) + dot(al, bh, dims))


def fitted(fun, degree):
    x = np.cos(np.pi * (np.arange(400) + 0.5) / 400) * 0.125 + 0.125
    series = np.polynomial.chebyshev.Chebyshev.fit(x, fun(x), degree, domain=[0, 0.25])
    return [float(v) for v in series.convert(kind=np.polynomial.Polynomial).coef]


SINE = fitted(lambda y: np.sin(2 * np.pi * np.sqrt(y)) / np.sqrt(y), 7)
COSINE = fitted(lambda y: np.cos(2 * np.pi * np.sqrt(y)), 7)


def horner(x, coefs):
    acc = coefs[-1]
    for c in coefs[-2::-1]:
        acc = acc * x + c
    return acc


def sincos_turns(t):
    f = t - jnp.round(t)
    f2 = f * f
    return f * horner(f2, SINE), horner(f2, COSINE)


def select(mask, rows):
    zero = jnp.zeros((), BF16)
    return jnp.concatenate([jnp.where(mask, r.astype(BF16), zero) for r in rows], axis=0)


def moments(mask, gv, ux, uy, uz):
    gx, gy = gv * ux, gv * uy
    return select(mask, [gv, gx, gy, gv * uz, gx * uy, gx * ux - gy * uy])


def left_operand(s, scale):
    one, x, y, z, xy, xxyy = [s[:128, 128 * j : 128 * (j + 1)] * scale for j in range(6)]
    zx, zy, zz = [s[128:, 128 * j : 128 * (j + 1)] * scale for j in (1, 2, 3)]
    k = 1.732
    e4, e5, e6, e7, e8 = (k * k) * xy, (k * k) * zy, (k * k) * zx, (k * 0.866) * xxyy, 1.5 * zz - 0.5 * one
    return jnp.concatenate(
        [
            jnp.concatenate([one - 0.5 * e8, 0.5 * x, 0.5 * y, 0.5 * z], axis=1),
            jnp.concatenate([x, e7, e4, e6], axis=1),
            jnp.concatenate([y, e4, -e7, e5], axis=1),
            jnp.concatenate([z, e6, e5, 3.0 * e8], axis=1),
        ],
        axis=0,
    ).astype(BF16)


def offset_list():
    cells = [(a, b, c) for a in (-1, 0, 1) for b in (-1, 0, 1) for c in (-1, 0, 1) if a or b or c]
    return sorted(cells, key=lambda o: abs(o[0]) + abs(o[1]) + abs(o[2]))


def blocks():
    out, start = [], 0
    for o in offset_list():
        width = (32, 8, 8)[abs(o[0]) + abs(o[1]) + abs(o[2]) - 1]
        out.append((o, start, width))
        start += width
    return out


def partner(offset, sign, sizes):
    at = [lax.axis_index(a) for a in ("gx", "gy", "gz")]
    return tuple(lax.rem(i + sign * o + n, n) for i, o, n in zip(at, offset, sizes))


def greet(sizes):
    barrier = pltpu.get_barrier_semaphore()
    for o in offset_list():
        pl.semaphore_signal(barrier, inc=1, device_id=partner(o, 1, sizes), device_id_type=MESH)


def greeted():
    pl.semaphore_wait(pltpu.get_barrier_semaphore(), 26)


def exchange(src, dst, send, recv, sign, sizes):
    def copy(rows, offset):
        return pltpu.make_async_remote_copy(
            src_ref=src.at[rows],
            dst_ref=dst.at[rows],
            send_sem=send,
            recv_sem=recv,
            device_id=partner(offset, sign, sizes),
            device_id_type=MESH,
        )

    for offset, start, rows in reversed(blocks()):
        copy(pl.ds(start, rows), offset).start()
    return copy(pl.ds(0, GHOSTS), blocks()[0][0])


def lanes_to_rows(x, rows):
    x = jnp.concatenate([x, jnp.zeros((120, x.shape[1]), F32)], axis=0)
    if x.shape[1] % 128:
        x = jnp.concatenate([x, jnp.zeros((128, -x.shape[1] % 128), F32)], axis=1)
    return x.T[:rows]


def rows_to_lanes(x):
    n = x.shape[0]
    if n % 128:
        x = jnp.concatenate([x, jnp.zeros((-n % 128, 128), F32)], axis=0)
    return x.T[:, :n]


def staggered(make, count):
    live = []
    for k in range(count):
        live.append(make(k))
        live = [x for x in live if advance(x)]
    while live:
        live = [x for x in live if advance(x)]


def advance(x):
    try:
        next(x)
    except StopIteration:
        return False
    return True


def total(parts):
    return functools.reduce(jnp.add, parts)


def kernel(
    sizes,
    count_ref,
    pos_hbm,
    feat_hbm,
    face_hbm,
    edge_hbm,
    corner_hbm,
    centre_hbm,
    other_hbm,
    wpa_hbm,
    wpb_hbm,
    wr_hbm,
    w1_hbm,
    we_hbm,
    wv_hbm,
    w2_hbm,
    wout_ref,
    small_ref,
    fgrad_ref,
    pos_ref,
    feat_ref,
    face_ref,
    edge_ref,
    corner_ref,
    centre_ref,
    other_ref,
    wpa_ref,
    wpb_ref,
    wr_ref,
    w1_ref,
    we_ref,
    wv_ref,
    w2_ref,
    out_s,
    in_s,
    ret_s,
    oh_s,
    p_s,
    first_s,
    slope_s,
    q_s,
    v_s,
    ds2_s,
    dv_s,
    final_s,
    saved_s,
    acc_s,
    rows_s,
    bp_s,
    send_a,
    recv_a,
    send_b,
    recv_b,
    load,
):
    edges = centre_ref.shape[1]
    width = WIDTH
    pairs = [
        (feat_hbm, feat_ref),
        (wpb_hbm, wpb_ref),
        (w1_hbm, w1_ref),
        (pos_hbm, pos_ref),
        (face_hbm, face_ref),
        (edge_hbm, edge_ref),
        (corner_hbm, corner_ref),
        (centre_hbm, centre_ref),
        (other_hbm, other_ref),
        (wpa_hbm, wpa_ref),
        (wr_hbm, wr_ref),
        (we_hbm, we_ref),
        (wv_hbm, wv_ref),
        (w2_hbm, w2_ref),
    ]
    loads = [pltpu.make_async_copy(src, dst, load.at[k]) for k, (src, dst) in enumerate(pairs)]
    for copy in loads[:7]:
        copy.start()
    greet(sizes)
    for copy in loads[7:]:
        copy.start()
    for copy in loads[:7]:
        copy.wait()

    feat = feat_ref[...]
    w1 = w1_ref[...]
    w1b = sum(dot(x, w1) for x in split(wpb_ref[...], 3))
    pb = dot32(feat, w1b)
    pos = jnp.concatenate([pos_ref[...], jnp.zeros((5, 128), F32)], axis=0)
    edge = jnp.concatenate([edge_ref[0].astype(F32), jnp.zeros((8, 116), F32)], axis=1)
    corner = jnp.concatenate([corner_ref[0].astype(F32), jnp.full((6, 8), -1.0, F32)], axis=0)
    corner = jnp.concatenate([corner, jnp.zeros((8, 120), F32)], axis=1)
    lists = jnp.concatenate([edge, corner, jnp.zeros((112, 128), F32)], axis=0).T.astype(jnp.int32)
    pieces = [face_ref[k] for k in range(6)] + [lists[k : k + 1, 0:8] for k in range(12)]
    pieces += [lists[k : k + 1, 8:16] for k in range(8)]
    slots = jnp.concatenate(pieces, axis=1)
    pick = (lax.broadcasted_iota(jnp.int32, (128, GHOSTS), 0) == slots).astype(F32).astype(BF16)
    out_s[:, 0:128] = dot(pick, pb.astype(BF16), TN)
    low = dot(jnp.concatenate([p.astype(F32) for p in split(pos, 3)], axis=0).astype(BF16), pick)
    out_s[:, 128:256] = lanes_to_rows(low[0:8] + low[8:16] + low[16:24], GHOSTS)
    greeted()
    ghosts = exchange(out_s, in_s, send_a, recv_a, 1, sizes)
    for copy in loads[7:]:
        copy.wait()

    iota = lax.broadcasted_iota(jnp.int32, (128, edges), 0).astype(F32).astype(BF16)
    one, zero = jnp.ones((), BF16), jnp.zeros((), BF16)
    cb = centre_ref[...].astype(F32).astype(BF16)
    o = other_ref[...]
    far = jnp.maximum(o - 416, 0)
    o = jnp.where(o < 416, o, 416 + (far >> 1) * 8 + (far & 1))
    oh_s[0:128, :] = jnp.where(iota == cb, one, zero)
    for t in range(4):
        n = 128 if t < 3 else 96
        ob = (o - 128 * t).astype(F32).astype(BF16)
        oh_s[128 * (t + 1) : 128 * (t + 1) + n, :] = jnp.where(iota[:n] == ob, one, zero)
    w1a = sum(dot(x, w1) for x in split(wpa_ref[...], 3))
    pa = dot32(feat, w1a)
    table = jnp.concatenate([pa.T, pb.T], axis=1).astype(BF16)
    both = jnp.concatenate([-pos, pos], axis=1)
    places = [p.astype(F32) for p in split(both, 3)]
    places = jnp.concatenate(places + [jnp.zeros_like(both)], axis=0).astype(BF16)
    p_s[...] = dot(jnp.concatenate([table, places], axis=0), oh_s[0:256, :])
    wevt = jnp.concatenate([we_ref[...].astype(F32).T, wv_ref[...].astype(F32).T], axis=0).astype(BF16)
    w2 = w2_ref[...]
    w2t = w2.astype(F32).T.astype(BF16)
    wback = jnp.concatenate([w2[:128], wv_ref[...], we_ref[...]], axis=1)
    w2b = w2[128:]
    wr = sum(dot(x, w1) for x in split(jnp.concatenate([wr_ref[...], jnp.zeros((8, 128), F32)], axis=0), 3))[:8]
    wr_hi = wr.astype(BF16).astype(F32)
    wr_lo = wr - wr_hi
    wrt = jnp.concatenate([wr_hi, wr_lo, wr_hi, jnp.zeros((104, 128), F32)], axis=0).T[:, :32].astype(BF16)
    wr2 = jnp.concatenate([wr_hi, wr_lo], axis=0).astype(BF16)
    wout = jnp.broadcast_to(wout_ref[...].astype(F32), (128, 128)).T
    wout = jnp.concatenate([wout] * (edges // 128), axis=1)
    count = count_ref[0]

    ghosts.wait()
    got = in_s[...]
    gpos = rows_to_lanes(got[:, 128:])[:8]
    places = [p.astype(F32) for p in split(gpos, 3)]
    places = jnp.concatenate(places + [jnp.zeros_like(gpos)], axis=0).astype(BF16)
    table = jnp.concatenate([rows_to_lanes(got[:, :128]).astype(BF16), places], axis=0)

    def group(k):
        at = slice(k * width, (k + 1) * width)
        cols = pl.ds(k * width, width)

        p = p_s[:, cols] + dot(table, oh_s[256:ROWS, cols])
        yield
        disp = p[128:136] + p[136:144] + p[144:152]
        dx, dy, dz = disp[0:1], disp[1:2], disp[2:3]
        sq = dx * dx + dy * dy + dz * dz + 0.01
        inv = lax.rsqrt(sq)
        dist = sq * inv
        ux, uy, uz = dx * inv, dy * inv, dz * inv
        is4 = 1.0 / (1.0 + 0.25 * dist * dist)
        g = is4 * is4
        gd = -dist * g * is4
        lane = lax.broadcasted_iota(jnp.int32, (1, width), 1) + k * width
        valid = jnp.where(lane < count, 1.0, 0.0)
        gv = g * valid
        h = g * inv
        hd = (gd - h) * inv
        order = lax.broadcasted_iota(jnp.int32, (8, width), 0).astype(F32) + 1.0
        sn, cs = sincos_turns(order * (0.25 * dist))
        basis = sn * h
        bp_s[:, cols] = order * (math.pi / 2) * cs * h + sn * hd
        rows_s[:, cols] = jnp.concatenate([ux, uy, uz, gv, inv, valid, gd, jnp.zeros_like(gd)], axis=0)
        b_hi = basis.astype(BF16).astype(F32)
        b4 = jnp.concatenate([b_hi, b_hi, basis - b_hi, jnp.zeros_like(basis)], axis=0).astype(BF16)
        z1 = p[:128] + dot(wrt, b4)
        yield
        sg = 0.5 * jnp.tanh(0.5 * z1) + 0.5
        f = z1 * sg
        first = f.astype(BF16)
        first_s[:, cols] = first
        slope_s[:, cols] = ((sg + f * (1.0 - sg)) * gv).astype(BF16)
        qv = dot(wevt, first)
        yield
        q_s[:, cols] = qv[:128].astype(BF16)
        v_s[:, cols] = qv[128:].astype(BF16)
        mask = iota[:, at] == cb[:, at]
        pair = jnp.concatenate([qv[:128].astype(BF16), (qv[:128] * uz).astype(BF16)], axis=0)
        env.append(dot(pair, moments(mask, gv, ux, uy, uz), NT))

    def group_b(k):
        at = slice(k * width, (k + 1) * width)
        cols = pl.ds(k * width, width)
        rows = rows_s[:, cols]
        ux, uy, uz, gv = rows[0:1], rows[1:2], rows[2:3], rows[3:4]
        mask = iota[:, at] == cb[:, at]
        t4 = dot(left, select(mask, [jnp.ones_like(ux), ux, uy, uz]))
        yield
        tx, ty, tz = t4[128:256], t4[256:384], t4[384:512]
        t = t4[:128] + (0.5 * ux) * tx + (0.5 * uy) * ty + (0.5 * uz) * tz
        vf = v_s[:, cols].astype(F32)
        z2 = dot(w2t, jnp.concatenate([first_s[:, cols], (vf * t).astype(BF16)], axis=0))
        yield
        sg = 0.5 * jnp.tanh(0.5 * z2) + 0.5
        f = z2 * sg
        eo = jnp.sum(f.astype(BF16).astype(F32) * wout[:, at], axis=0, keepdims=True)
        ds2 = (wout[:, at] * (sg + f * (1.0 - sg))).astype(BF16)
        ds2_s[:, cols] = ds2
        dsc = dot(w2b, ds2)
        yield
        dv_s[:, cols] = (t * dsc).astype(BF16)
        y = vf * dsc
        du = [jnp.sum(y * c, axis=0, keepdims=True) for c in (tx, ty, tz)]
        saved_s[:, cols] = jnp.concatenate(du + [eo, jnp.zeros((4, width), F32)], axis=0)
        pair = jnp.concatenate([y.astype(BF16), (y * uz).astype(BF16)], axis=0)
        env.append(dot(pair, moments(mask, gv, ux, uy, uz), NT))

    def group_c(k):
        at = slice(k * width, (k + 1) * width)
        cols = pl.ds(k * width, width)
        rows = rows_s[:, cols]
        ux, uy, uz, gv = rows[0:1], rows[1:2], rows[2:3], rows[3:4]
        mask = iota[:, at] == cb[:, at]
        d4 = dot(left, select(mask, [jnp.ones_like(ux), ux, uy, uz]))
        yield
        kx, ky, kz = d4[128:256], d4[256:384], d4[384:512]
        d = d4[:128] + (0.5 * ux) * kx + (0.5 * uy) * ky + (0.5 * uz) * kz
        qf = q_s[:, cols].astype(F32)
        saved = saved_s[:, cols]
        dux, duy, duz = [saved[j : j + 1] + jnp.sum(qf * c, axis=0, keepdims=True) for j, c in enumerate((kx, ky, kz))]
        dgq = jnp.sum(qf * d, axis=0, keepdims=True)
        df = dot(wback, jnp.concatenate([ds2_s[:, cols], dv_s[:, cols], d.astype(BF16)], axis=0))
        yield
        dz1 = (df * slope_s[:, cols].astype(F32)).astype(BF16)
        db = dot(wr2, dz1)
        yield
        db = db[:8] + db[8:]
        inv, valid, gd = rows[4:5], rows[5:6], rows[6:7]
        dux, duy, duz = gv * dux, gv * duy, gv * duz
        eo = saved[3:4]
        dd = jnp.sum(db * bp_s[:, cols], axis=0, keepdims=True) + valid * (eo + dgq) * gd
        dd = dd - (dux * ux + duy * uy + duz * uz) * inv
        tail = [dux * inv + dd * ux, duy * inv + dd * uy, duz * inv + dd * uz, eo * gv, jnp.zeros((4, width), F32)]
        tail = jnp.concatenate(tail, axis=0)
        tail_hi = tail.astype(BF16).astype(F32)
        low = jnp.concatenate([tail_hi, tail - tail_hi], axis=0).astype(BF16)
        final = jnp.concatenate([dz1, low], axis=0)
        final_s[:, cols] = final
        env.append(dot(oh_s[256:ROWS, cols], final, NT))

    env = []
    staggered(group, edges // width)
    left = left_operand(total(env), 0.2)
    env = []
    staggered(group_b, edges // width)
    left = left_operand(total(env), 0.2)
    env = []
    staggered(group_c, edges // width)

    acc = total(env)
    out_s[:, 0:128] = acc[:, :128]
    out_s[:, 128:256] = jnp.concatenate([acc[:, 128:136] + acc[:, 136:144], jnp.zeros((GHOSTS, 120), F32)], axis=1)
    returns = exchange(out_s, ret_s, send_b, recv_b, -1, sizes)
    acc_s[...] = jnp.zeros_like(acc_s)

    def owned(k, carry):
        cols = pl.ds(pl.multiple_of(k * (edges // 2), 128), edges // 2)
        acc_s[...] += dot(oh_s[0:256, cols], final_s[:, cols], NT)
        return carry

    lax.fori_loop(0, 2, owned, 0)
    acc = acc_s[...]
    low = acc[:, 128:136] + acc[:, 136:144]
    low = jnp.concatenate([low, jnp.zeros((256, 120), F32)], axis=1).T[:8]
    part = dot32(acc[:128, :128], w1a, NT)
    own = acc[128:, :128]
    returns.wait()
    got = ret_s[...]
    a_hi, a_lo = split(got[:, :128], 2)
    own = own + (dot(pick, a_hi) + dot(pick, a_lo))
    back = [dot(pick, x) for x in split(got[:, 128:], 3)]
    back = (back[0] + back[1] + back[2]).T[:8]
    fgrad_ref[...] = part + dot32(own, w1b, NT)
    small_ref[...] = jnp.concatenate([low[0:3, :128] - low[0:3, 128:] - back[0:3], low[3:8, :128]], axis=0)


def place(small_ref, wide_ref, force_ref, energy_ref, fgrad_ref):
    force_ref[...] = small_ref[0:3, :]
    energy_ref[...] = small_ref[3:4, :]
    fgrad_ref[...] = wide_ref[...]


def local(
    sizes,
    positions,
    atom_features,
    send_face,
    send_edge,
    send_corner,
    centre,
    other,
    edge_count,
    w_proj_a,
    w_proj_b,
    w_radial,
    w_first,
    w_env,
    w_value,
    w_second,
    w_out,
):
    vm = pl.BlockSpec(memory_space=pltpu.VMEM)
    edges = centre.shape[0]
    operands = [
        positions,
        atom_features,
        jnp.transpose(send_face, (1, 0, 2)),
        jnp.transpose(send_edge, (0, 2, 1)),
        jnp.transpose(send_corner, (0, 2, 1)),
        centre.reshape(1, -1),
        other.reshape(1, -1),
        w_proj_a,
        w_proj_b,
        w_radial,
        w_first,
        w_env,
        w_value,
        w_second,
        w_out.reshape(1, -1),
    ]
    small, wide = pl.pallas_call(
        functools.partial(kernel, sizes),
        out_shape=[jax.ShapeDtypeStruct((8, 128), F32), jax.ShapeDtypeStruct((128, 128), F32)],
        in_specs=[pl.BlockSpec(memory_space=pltpu.SMEM)] + [pl.BlockSpec(memory_space=pl.ANY)] * 14 + [vm],
        out_specs=[vm] * 2,
        scratch_shapes=[pltpu.VMEM(x.shape, x.dtype) for x in operands[:14]]
        + [
            pltpu.VMEM((GHOSTS, 256), F32),
            pltpu.VMEM((GHOSTS, 256), F32),
            pltpu.VMEM((GHOSTS, 256), F32),
            pltpu.VMEM((ROWS, edges), BF16),
            pltpu.VMEM((160, edges), F32),
            *[pltpu.VMEM((128, edges), BF16)] * 6,
            pltpu.VMEM((144, edges), BF16),
            pltpu.VMEM((8, edges), F32),
            pltpu.VMEM((256, 144), F32),
            pltpu.VMEM((8, edges), F32),
            pltpu.VMEM((8, edges), F32),
        ]
        + [pltpu.SemaphoreType.DMA(())] * 4
        + [pltpu.SemaphoreType.DMA((14,))],
        compiler_params=pltpu.CompilerParams(
            collective_id=0, has_side_effects=True, vmem_limit_bytes=60 * 2**20
        ),
    )(edge_count, *operands)
    force, energy, fgrad = pl.pallas_call(
        place,
        out_shape=[
            jax.ShapeDtypeStruct((3, 128), F32),
            jax.ShapeDtypeStruct((1, 128), F32),
            jax.ShapeDtypeStruct((128, 128), F32),
        ],
        in_specs=[vm] * 2,
        out_specs=[vm] * 3,
    )(small, wide)
    return force, energy.reshape(-1), fgrad


def solution(mesh):
    axes = ("gx", "gy", "gz")
    sizes = tuple(mesh.shape[a] for a in axes)
    split_first = [P(axes, None), P(axes, None, None), P(axes, None, None), P(axes, None, None)]
    return jax.shard_map(
        functools.partial(local, sizes),
        mesh=mesh,
        in_specs=(P(None, axes), *split_first, P(axes), P(axes), P(axes)) + (P(),) * 8,
        out_specs=(P(None, axes), P(axes), P(axes, None)),
        check_vma=False,
    )
```

```python
import functools
import math

import jax
import jax.numpy as jnp
import numpy as np
from jax import lax
from jax.experimental import pallas as pl
from jax.experimental.pallas import tpu as pltpu
from jax.sharding import PartitionSpec as P

F32, BF16 = jnp.float32, jnp.bfloat16
MESH = pl.DeviceIdType.MESH
NN = (((1,), (0,)), ((), ()))
NT = (((1,), (1,)), ((), ()))
TN = (((0,), (0,)), ((), ()))
OWN = 128
GHOSTS = 352
ROWS = 2 * OWN + GHOSTS
WIDTHS = (512, 1024, 1024, 1024, 1024, 1024, 512)


def dot(a, b, dims=NN):
    return lax.dot_general(a, b, dims, preferred_element_type=F32)


def split(x, n):
    parts = []
    for _ in range(n):
        part = x.astype(BF16)
        parts.append(part)
        x = x - part.astype(F32)
    return parts


def dot32(a, b, dims=NN):
    (ah, al), (bh, bl) = split(a, 2), split(b, 2)
    return dot(ah, bh, dims) + (dot(ah, bl, dims) + dot(al, bh, dims))


def fitted(fun, degree):
    x = np.cos(np.pi * (np.arange(400) + 0.5) / 400) * 0.125 + 0.125
    series = np.polynomial.chebyshev.Chebyshev.fit(x, fun(x), degree, domain=[0, 0.25])
    return [float(v) for v in series.convert(kind=np.polynomial.Polynomial).coef]


SINE = fitted(lambda y: np.sin(2 * np.pi * np.sqrt(y)) / np.sqrt(y), 7)
COSINE = fitted(lambda y: np.cos(2 * np.pi * np.sqrt(y)), 7)


def horner(x, coefs):
    acc = coefs[-1]
    for c in coefs[-2::-1]:
        acc = acc * x + c
    return acc


def sincos_turns(t):
    f = t - jnp.round(t)
    f2 = f * f
    return f * horner(f2, SINE), horner(f2, COSINE)


def select(mask, rows):
    zero = jnp.zeros((), BF16)
    return jnp.concatenate([jnp.where(mask, r.astype(BF16), zero) for r in rows], axis=0)


def moments(mask, gv, ux, uy, uz):
    gx, gy = gv * ux, gv * uy
    return select(mask, [gv, gx, gy, gv * uz, gx * uy, gx * ux - gy * uy])


def left_operand(s, scale):
    one, x, y, z, xy, xxyy = [s[:128, 128 * j : 128 * (j + 1)] * scale for j in range(6)]
    zx, zy, zz = [s[128:, 128 * j : 128 * (j + 1)] * scale for j in (1, 2, 3)]
    k = 1.732
    e4, e5, e6, e7, e8 = (k * k) * xy, (k * k) * zy, (k * k) * zx, (k * 0.866) * xxyy, 1.5 * zz - 0.5 * one
    return jnp.concatenate(
        [
            jnp.concatenate([one - 0.5 * e8, 0.5 * x, 0.5 * y, 0.5 * z], axis=1),
            jnp.concatenate([x, e7, e4, e6], axis=1),
            jnp.concatenate([y, e4, -e7, e5], axis=1),
            jnp.concatenate([z, e6, e5, 3.0 * e8], axis=1),
        ],
        axis=0,
    ).astype(BF16)


def offset_list():
    cells = [(a, b, c) for a in (-1, 0, 1) for b in (-1, 0, 1) for c in (-1, 0, 1) if a or b or c]
    return sorted(cells, key=lambda o: abs(o[0]) + abs(o[1]) + abs(o[2]))


def blocks():
    out, start = [], 0
    for o in offset_list():
        width = (32, 8, 8)[abs(o[0]) + abs(o[1]) + abs(o[2]) - 1]
        out.append((o, start, width))
        start += width
    return out


def partner(offset, sign, sizes):
    at = [lax.axis_index(a) for a in ("gx", "gy", "gz")]
    return tuple(lax.rem(i + sign * o + n, n) for i, o, n in zip(at, offset, sizes))


def greet(sizes):
    barrier = pltpu.get_barrier_semaphore()
    for o in offset_list():
        pl.semaphore_signal(barrier, inc=1, device_id=partner(o, 1, sizes), device_id_type=MESH)


def greeted():
    pl.semaphore_wait(pltpu.get_barrier_semaphore(), 26)


def exchange(src, dst, send, recv, sign, sizes):
    def copy(rows, offset):
        return pltpu.make_async_remote_copy(
            src_ref=src.at[rows],
            dst_ref=dst.at[rows],
            send_sem=send,
            recv_sem=recv,
            device_id=partner(offset, sign, sizes),
            device_id_type=MESH,
        )

    for offset, start, rows in reversed(blocks()):
        copy(pl.ds(start, rows), offset).start()
    return copy(pl.ds(0, GHOSTS), blocks()[0][0])


def lanes_to_rows(x, rows):
    x = jnp.concatenate([x, jnp.zeros((120, x.shape[1]), F32)], axis=0)
    if x.shape[1] % 128:
        x = jnp.concatenate([x, jnp.zeros((128, -x.shape[1] % 128), F32)], axis=1)
    return x.T[:rows]


def rows_to_lanes(x):
    n = x.shape[0]
    if n % 128:
        x = jnp.concatenate([x, jnp.zeros((-n % 128, 128), F32)], axis=0)
    return x.T[:, :n]


def staggered(make, widths):
    live, start = [], 0
    for width in widths:
        live.append(make(start, width))
        start += width
        live = [x for x in live if advance(x)]
    while live:
        live = [x for x in live if advance(x)]


def advance(x):
    try:
        next(x)
    except StopIteration:
        return False
    return True


def total(parts):
    return functools.reduce(jnp.add, parts)


def kernel(
    sizes,
    count_ref,
    pos_hbm,
    feat_hbm,
    face_hbm,
    edge_hbm,
    corner_hbm,
    centre_hbm,
    other_hbm,
    wpa_hbm,
    wpb_hbm,
    wr_hbm,
    w1_hbm,
    we_hbm,
    wv_hbm,
    w2_hbm,
    wout_ref,
    small_ref,
    fgrad_ref,
    pos_ref,
    feat_ref,
    face_ref,
    edge_ref,
    corner_ref,
    centre_ref,
    other_ref,
    wpa_ref,
    wpb_ref,
    wr_ref,
    w1_ref,
    we_ref,
    wv_ref,
    w2_ref,
    out_s,
    in_s,
    ret_s,
    oh_s,
    p_s,
    first_s,
    slope_s,
    q_s,
    v_s,
    ds2_s,
    dv_s,
    final_s,
    saved_s,
    acc_s,
    rows_s,
    bp_s,
    send_a,
    recv_a,
    send_b,
    recv_b,
    load,
):
    edges = centre_ref.shape[1]
    pairs = [
        (feat_hbm, feat_ref),
        (wpb_hbm, wpb_ref),
        (w1_hbm, w1_ref),
        (pos_hbm, pos_ref),
        (face_hbm, face_ref),
        (edge_hbm, edge_ref),
        (corner_hbm, corner_ref),
        (centre_hbm, centre_ref),
        (other_hbm, other_ref),
        (wpa_hbm, wpa_ref),
        (wr_hbm, wr_ref),
        (we_hbm, we_ref),
        (wv_hbm, wv_ref),
        (w2_hbm, w2_ref),
    ]
    loads = [pltpu.make_async_copy(src, dst, load.at[k]) for k, (src, dst) in enumerate(pairs)]
    for copy in loads[:7]:
        copy.start()
    greet(sizes)
    for copy in loads[7:]:
        copy.start()
    for copy in loads[:7]:
        copy.wait()

    feat = feat_ref[...]
    w1 = w1_ref[...]
    w1b = sum(dot(x, w1) for x in split(wpb_ref[...], 3))
    pb = dot32(feat, w1b)
    pos = jnp.concatenate([pos_ref[...], jnp.zeros((5, 128), F32)], axis=0)
    edge = jnp.concatenate([edge_ref[0].astype(F32), jnp.zeros((8, 116), F32)], axis=1)
    corner = jnp.concatenate([corner_ref[0].astype(F32), jnp.full((6, 8), -1.0, F32)], axis=0)
    corner = jnp.concatenate([corner, jnp.zeros((8, 120), F32)], axis=1)
    lists = jnp.concatenate([edge, corner, jnp.zeros((112, 128), F32)], axis=0).T.astype(jnp.int32)
    pieces = [face_ref[k] for k in range(6)] + [lists[k : k + 1, 0:8] for k in range(12)]
    pieces += [lists[k : k + 1, 8:16] for k in range(8)]
    slots = jnp.concatenate(pieces, axis=1)
    pick = (lax.broadcasted_iota(jnp.int32, (128, GHOSTS), 0) == slots).astype(F32).astype(BF16)
    out_s[:, 0:128] = dot(pick, pb.astype(BF16), TN)
    low = dot(jnp.concatenate([p.astype(F32) for p in split(pos, 3)], axis=0).astype(BF16), pick)
    out_s[:, 128:256] = lanes_to_rows(low[0:8] + low[8:16] + low[16:24], GHOSTS)
    greeted()
    ghosts = exchange(out_s, in_s, send_a, recv_a, 1, sizes)
    for copy in loads[7:]:
        copy.wait()

    iota = lax.broadcasted_iota(jnp.int32, (128, edges), 0).astype(F32).astype(BF16)
    one, zero = jnp.ones((), BF16), jnp.zeros((), BF16)
    cb = centre_ref[...].astype(F32).astype(BF16)
    o = other_ref[...]
    far = jnp.maximum(o - 416, 0)
    o = jnp.where(o < 416, o, 416 + (far >> 1) * 8 + (far & 1))
    oh_s[0:128, :] = jnp.where(iota == cb, one, zero)
    for t in range(4):
        n = 128 if t < 3 else 96
        ob = (o - 128 * t).astype(F32).astype(BF16)
        oh_s[128 * (t + 1) : 128 * (t + 1) + n, :] = jnp.where(iota[:n] == ob, one, zero)
    w1a = sum(dot(x, w1) for x in split(wpa_ref[...], 3))
    pa = dot32(feat, w1a)
    table = jnp.concatenate([pa.T, pb.T], axis=1).astype(BF16)
    both = jnp.concatenate([-pos, pos], axis=1)
    places = [p.astype(F32) for p in split(both, 3)]
    places = jnp.concatenate(places + [jnp.zeros_like(both)], axis=0).astype(BF16)
    p_s[...] = dot(jnp.concatenate([table, places], axis=0), oh_s[0:256, :])
    wevt = jnp.concatenate([we_ref[...].astype(F32).T, wv_ref[...].astype(F32).T], axis=0).astype(BF16)
    w2 = w2_ref[...]
    w2t = w2.astype(F32).T.astype(BF16)
    wback = jnp.concatenate([w2[:128], wv_ref[...], we_ref[...]], axis=1)
    w2b = w2[128:]
    wr = sum(dot(x, w1) for x in split(jnp.concatenate([wr_ref[...], jnp.zeros((8, 128), F32)], axis=0), 3))[:8]
    wr_hi = wr.astype(BF16).astype(F32)
    wr_lo = wr - wr_hi
    wrt = jnp.concatenate([wr_hi, wr_lo, wr_hi, jnp.zeros((104, 128), F32)], axis=0).T[:, :32].astype(BF16)
    wr2 = jnp.concatenate([wr_hi, wr_lo], axis=0).astype(BF16)
    wout = jnp.broadcast_to(wout_ref[...].astype(F32), (128, 128)).T
    wout = jnp.concatenate([wout] * (edges // 128), axis=1)
    count = count_ref[0]

    ghosts.wait()
    got = in_s[...]
    gpos = rows_to_lanes(got[:, 128:])[:8]
    places = [p.astype(F32) for p in split(gpos, 3)]
    places = jnp.concatenate(places + [jnp.zeros_like(gpos)], axis=0).astype(BF16)
    table = jnp.concatenate([rows_to_lanes(got[:, :128]).astype(BF16), places], axis=0)

    def group(start, width):
        at = slice(start, start + width)
        cols = pl.ds(start, width)

        p = p_s[:, cols] + dot(table, oh_s[256:ROWS, cols])
        yield
        disp = p[128:136] + p[136:144] + p[144:152]
        dx, dy, dz = disp[0:1], disp[1:2], disp[2:3]
        sq = dx * dx + dy * dy + dz * dz + 0.01
        inv = lax.rsqrt(sq)
        dist = sq * inv
        ux, uy, uz = dx * inv, dy * inv, dz * inv
        is4 = 1.0 / (1.0 + 0.25 * dist * dist)
        g = is4 * is4
        gd = -dist * g * is4
        lane = lax.broadcasted_iota(jnp.int32, (1, width), 1) + start
        valid = jnp.where(lane < count, 1.0, 0.0)
        gv = g * valid
        h = g * inv
        hd = (gd - h) * inv
        order = lax.broadcasted_iota(jnp.int32, (8, width), 0).astype(F32) + 1.0
        sn, cs = sincos_turns(order * (0.25 * dist))
        basis = sn * h
        bp_s[:, cols] = order * (math.pi / 2) * cs * h + sn * hd
        rows_s[:, cols] = jnp.concatenate([ux, uy, uz, gv, inv, valid, gd, jnp.zeros_like(gd)], axis=0)
        b_hi = basis.astype(BF16).astype(F32)
        b4 = jnp.concatenate([b_hi, b_hi, basis - b_hi, jnp.zeros_like(basis)], axis=0).astype(BF16)
        z1 = p[:128] + dot(wrt, b4)
        yield
        sg = 0.5 * jnp.tanh(0.5 * z1) + 0.5
        f = z1 * sg
        first = f.astype(BF16)
        first_s[:, cols] = first
        slope_s[:, cols] = ((sg + f * (1.0 - sg)) * gv).astype(BF16)
        qv = dot(wevt, first)
        yield
        q_s[:, cols] = qv[:128].astype(BF16)
        v_s[:, cols] = qv[128:].astype(BF16)
        mask = iota[:, at] == cb[:, at]
        pair = jnp.concatenate([qv[:128].astype(BF16), (qv[:128] * uz).astype(BF16)], axis=0)
        env.append(dot(pair, moments(mask, gv, ux, uy, uz), NT))

    def group_b(start, width):
        at = slice(start, start + width)
        cols = pl.ds(start, width)
        rows = rows_s[:, cols]
        ux, uy, uz, gv = rows[0:1], rows[1:2], rows[2:3], rows[3:4]
        mask = iota[:, at] == cb[:, at]
        t4 = dot(left, select(mask, [jnp.ones_like(ux), ux, uy, uz]))
        yield
        tx, ty, tz = t4[128:256], t4[256:384], t4[384:512]
        t = t4[:128] + (0.5 * ux) * tx + (0.5 * uy) * ty + (0.5 * uz) * tz
        vf = v_s[:, cols].astype(F32)
        z2 = dot(w2t, jnp.concatenate([first_s[:, cols], (vf * t).astype(BF16)], axis=0))
        yield
        sg = 0.5 * jnp.tanh(0.5 * z2) + 0.5
        f = z2 * sg
        eo = jnp.sum(f.astype(BF16).astype(F32) * wout[:, at], axis=0, keepdims=True)
        ds2 = (wout[:, at] * (sg + f * (1.0 - sg))).astype(BF16)
        ds2_s[:, cols] = ds2
        dsc = dot(w2b, ds2)
        yield
        dv_s[:, cols] = (t * dsc).astype(BF16)
        y = vf * dsc
        du = [jnp.sum(y * c, axis=0, keepdims=True) for c in (tx, ty, tz)]
        saved_s[:, cols] = jnp.concatenate(du + [eo, jnp.zeros((4, width), F32)], axis=0)
        pair = jnp.concatenate([y.astype(BF16), (y * uz).astype(BF16)], axis=0)
        env.append(dot(pair, moments(mask, gv, ux, uy, uz), NT))

    def group_c(start, width):
        at = slice(start, start + width)
        cols = pl.ds(start, width)
        rows = rows_s[:, cols]
        ux, uy, uz, gv = rows[0:1], rows[1:2], rows[2:3], rows[3:4]
        mask = iota[:, at] == cb[:, at]
        d4 = dot(left, select(mask, [jnp.ones_like(ux), ux, uy, uz]))
        yield
        kx, ky, kz = d4[128:256], d4[256:384], d4[384:512]
        d = d4[:128] + (0.5 * ux) * kx + (0.5 * uy) * ky + (0.5 * uz) * kz
        qf = q_s[:, cols].astype(F32)
        saved = saved_s[:, cols]
        dux, duy, duz = [saved[j : j + 1] + jnp.sum(qf * c, axis=0, keepdims=True) for j, c in enumerate((kx, ky, kz))]
        dgq = jnp.sum(qf * d, axis=0, keepdims=True)
        df = dot(wback, jnp.concatenate([ds2_s[:, cols], dv_s[:, cols], d.astype(BF16)], axis=0))
        yield
        dz1 = (df * slope_s[:, cols].astype(F32)).astype(BF16)
        db = dot(wr2, dz1)
        yield
        db = db[:8] + db[8:]
        inv, valid, gd = rows[4:5], rows[5:6], rows[6:7]
        dux, duy, duz = gv * dux, gv * duy, gv * duz
        eo = saved[3:4]
        dd = jnp.sum(db * bp_s[:, cols], axis=0, keepdims=True) + valid * (eo + dgq) * gd
        dd = dd - (dux * ux + duy * uy + duz * uz) * inv
        tail = [dux * inv + dd * ux, duy * inv + dd * uy, duz * inv + dd * uz, eo * gv, jnp.zeros((4, width), F32)]
        tail = jnp.concatenate(tail, axis=0)
        tail_hi = tail.astype(BF16).astype(F32)
        low = jnp.concatenate([tail_hi, tail - tail_hi], axis=0).astype(BF16)
        final = jnp.concatenate([dz1, low], axis=0)
        final_s[:, cols] = final
        env.append(dot(oh_s[256:ROWS, cols], final, NT))

    env = []
    staggered(group, WIDTHS)
    left = left_operand(total(env), 0.2)
    env = []
    staggered(group_b, WIDTHS)
    left = left_operand(total(env), 0.2)
    env = []
    staggered(group_c, WIDTHS)

    acc = total(env)
    out_s[:, 0:128] = acc[:, :128]
    out_s[:, 128:256] = jnp.concatenate([acc[:, 128:136] + acc[:, 136:144], jnp.zeros((GHOSTS, 120), F32)], axis=1)
    returns = exchange(out_s, ret_s, send_b, recv_b, -1, sizes)
    acc_s[...] = jnp.zeros_like(acc_s)

    def owned(k, carry):
        cols = pl.ds(pl.multiple_of(k * (edges // 2), 128), edges // 2)
        acc_s[...] += dot(oh_s[0:256, cols], final_s[:, cols], NT)
        return carry

    lax.fori_loop(0, 2, owned, 0)
    acc = acc_s[...]
    low = acc[:, 128:136] + acc[:, 136:144]
    low = jnp.concatenate([low, jnp.zeros((256, 120), F32)], axis=1).T[:8]
    part = dot32(acc[:128, :128], w1a, NT)
    own = acc[128:, :128]
    returns.wait()
    got = ret_s[...]
    a_hi, a_lo = split(got[:, :128], 2)
    own = own + (dot(pick, a_hi) + dot(pick, a_lo))
    back = [dot(pick, x) for x in split(got[:, 128:], 3)]
    back = (back[0] + back[1] + back[2]).T[:8]
    fgrad_ref[...] = part + dot32(own, w1b, NT)
    small_ref[...] = jnp.concatenate([low[0:3, :128] - low[0:3, 128:] - back[0:3], low[3:8, :128]], axis=0)


def place(small_ref, wide_ref, force_ref, energy_ref, fgrad_ref):
    force_ref[...] = small_ref[0:3, :]
    energy_ref[...] = small_ref[3:4, :]
    fgrad_ref[...] = wide_ref[...]


def local(
    sizes,
    positions,
    atom_features,
    send_face,
    send_edge,
    send_corner,
    centre,
    other,
    edge_count,
    w_proj_a,
    w_proj_b,
    w_radial,
    w_first,
    w_env,
    w_value,
    w_second,
    w_out,
):
    vm = pl.BlockSpec(memory_space=pltpu.VMEM)
    edges = centre.shape[0]
    operands = [
        positions,
        atom_features,
        jnp.transpose(send_face, (1, 0, 2)),
        jnp.transpose(send_edge, (0, 2, 1)),
        jnp.transpose(send_corner, (0, 2, 1)),
        centre.reshape(1, -1),
        other.reshape(1, -1),
        w_proj_a,
        w_proj_b,
        w_radial,
        w_first,
        w_env,
        w_value,
        w_second,
        w_out.reshape(1, -1),
    ]
    small, wide = pl.pallas_call(
        functools.partial(kernel, sizes),
        out_shape=[pltpu.VMEM((8, 128), F32), pltpu.VMEM((128, 128), F32)],
        in_specs=[pl.BlockSpec(memory_space=pltpu.SMEM)] + [pl.BlockSpec(memory_space=pl.ANY)] * 14 + [vm],
        out_specs=[vm] * 2,
        scratch_shapes=[pltpu.VMEM(x.shape, x.dtype) for x in operands[:14]]
        + [
            pltpu.VMEM((GHOSTS, 256), F32),
            pltpu.VMEM((GHOSTS, 256), F32),
            pltpu.VMEM((GHOSTS, 256), F32),
            pltpu.VMEM((ROWS, edges), BF16),
            pltpu.VMEM((160, edges), F32),
            *[pltpu.VMEM((128, edges), BF16)] * 6,
            pltpu.VMEM((144, edges), BF16),
            pltpu.VMEM((8, edges), F32),
            pltpu.VMEM((256, 144), F32),
            pltpu.VMEM((8, edges), F32),
            pltpu.VMEM((8, edges), F32),
        ]
        + [pltpu.SemaphoreType.DMA(())] * 4
        + [pltpu.SemaphoreType.DMA((14,))],
        compiler_params=pltpu.CompilerParams(
            collective_id=0, has_side_effects=True, vmem_limit_bytes=56 * 2**20
        ),
    )(edge_count, *operands)
    force, energy, fgrad = pl.pallas_call(
        place,
        out_shape=[
            jax.ShapeDtypeStruct((3, 128), F32),
            jax.ShapeDtypeStruct((1, 128), F32),
            jax.ShapeDtypeStruct((128, 128), F32),
        ],
        in_specs=[vm] * 2,
        out_specs=[vm] * 3,
    )(*[pltpu.with_memory_space_constraint(x, pltpu.VMEM) for x in (small, wide)])
    return force, energy.reshape(-1), fgrad


def solution(mesh):
    axes = ("gx", "gy", "gz")
    sizes = tuple(mesh.shape[a] for a in axes)
    split_first = [P(axes, None), P(axes, None, None), P(axes, None, None), P(axes, None, None)]
    return jax.shard_map(
        functools.partial(local, sizes),
        mesh=mesh,
        in_specs=(P(None, axes), *split_first, P(axes), P(axes), P(axes)) + (P(),) * 8,
        out_specs=(P(None, axes), P(axes), P(axes, None)),
        check_vma=False,
    )
```

```python
import functools
import math

import jax
import jax.numpy as jnp
import numpy as np
from jax import lax
from jax.experimental import pallas as pl
from jax.experimental.pallas import tpu as pltpu
from jax.sharding import PartitionSpec as P

F32, BF16 = jnp.float32, jnp.bfloat16
MESH = pl.DeviceIdType.MESH
NN = (((1,), (0,)), ((), ()))
NT = (((1,), (1,)), ((), ()))
TN = (((0,), (0,)), ((), ()))
OWN = 128
GHOSTS = 352
ROWS = 2 * OWN + GHOSTS
WIDTHS = (256, 768, 1024, 1024, 1024, 1024, 768, 256)


def dot(a, b, dims=NN):
    return lax.dot_general(a, b, dims, preferred_element_type=F32)


def split(x, n):
    parts = []
    for _ in range(n):
        part = x.astype(BF16)
        parts.append(part)
        x = x - part.astype(F32)
    return parts


def dot32(a, b, dims=NN):
    (ah, al), (bh, bl) = split(a, 2), split(b, 2)
    return dot(ah, bh, dims) + (dot(ah, bl, dims) + dot(al, bh, dims))


def fitted(fun, degree):
    x = np.cos(np.pi * (np.arange(400) + 0.5) / 400) * 0.125 + 0.125
    series = np.polynomial.chebyshev.Chebyshev.fit(x, fun(x), degree, domain=[0, 0.25])
    return [float(v) for v in series.convert(kind=np.polynomial.Polynomial).coef]


SINE = fitted(lambda y: np.sin(2 * np.pi * np.sqrt(y)) / np.sqrt(y), 7)
COSINE = fitted(lambda y: np.cos(2 * np.pi * np.sqrt(y)), 7)


def horner(x, coefs):
    acc = coefs[-1]
    for c in coefs[-2::-1]:
        acc = acc * x + c
    return acc


def sincos_turns(t):
    f = t - jnp.round(t)
    f2 = f * f
    return f * horner(f2, SINE), horner(f2, COSINE)


def select(mask, rows):
    zero = jnp.zeros((), BF16)
    return jnp.concatenate([jnp.where(mask, r.astype(BF16), zero) for r in rows], axis=0)


def moments(mask, gv, ux, uy, uz):
    gx, gy = gv * ux, gv * uy
    return select(mask, [gv, gx, gy, gv * uz, gx * uy, gx * ux - gy * uy])


def left_operand(s, scale):
    one, x, y, z, xy, xxyy = [s[:128, 128 * j : 128 * (j + 1)] * scale for j in range(6)]
    zx, zy, zz = [s[128:, 128 * j : 128 * (j + 1)] * scale for j in (1, 2, 3)]
    k = 1.732
    e4, e5, e6, e7, e8 = (k * k) * xy, (k * k) * zy, (k * k) * zx, (k * 0.866) * xxyy, 1.5 * zz - 0.5 * one
    return jnp.concatenate(
        [
            jnp.concatenate([one - 0.5 * e8, 0.5 * x, 0.5 * y, 0.5 * z], axis=1),
            jnp.concatenate([x, e7, e4, e6], axis=1),
            jnp.concatenate([y, e4, -e7, e5], axis=1),
            jnp.concatenate([z, e6, e5, 3.0 * e8], axis=1),
        ],
        axis=0,
    ).astype(BF16)


def offset_list():
    cells = [(a, b, c) for a in (-1, 0, 1) for b in (-1, 0, 1) for c in (-1, 0, 1) if a or b or c]
    return sorted(cells, key=lambda o: abs(o[0]) + abs(o[1]) + abs(o[2]))


def blocks():
    out, start = [], 0
    for o in offset_list():
        width = (32, 8, 8)[abs(o[0]) + abs(o[1]) + abs(o[2]) - 1]
        out.append((o, start, width))
        start += width
    return out


def partner(offset, sign, sizes):
    at = [lax.axis_index(a) for a in ("gx", "gy", "gz")]
    return tuple(lax.rem(i + sign * o + n, n) for i, o, n in zip(at, offset, sizes))


def greet(sizes):
    barrier = pltpu.get_barrier_semaphore()
    for o in offset_list():
        pl.semaphore_signal(barrier, inc=1, device_id=partner(o, 1, sizes), device_id_type=MESH)


def greeted():
    pl.semaphore_wait(pltpu.get_barrier_semaphore(), 26)


def exchange(src, dst, send, recv, sign, sizes):
    def copy(rows, offset):
        return pltpu.make_async_remote_copy(
            src_ref=src.at[rows],
            dst_ref=dst.at[rows],
            send_sem=send,
            recv_sem=recv,
            device_id=partner(offset, sign, sizes),
            device_id_type=MESH,
        )

    for offset, start, rows in reversed(blocks()):
        copy(pl.ds(start, rows), offset).start()
    return copy(pl.ds(0, GHOSTS), blocks()[0][0])


def lanes_to_rows(x, rows):
    x = jnp.concatenate([x, jnp.zeros((120, x.shape[1]), F32)], axis=0)
    if x.shape[1] % 128:
        x = jnp.concatenate([x, jnp.zeros((128, -x.shape[1] % 128), F32)], axis=1)
    return x.T[:rows]


def rows_to_lanes(x):
    n = x.shape[0]
    if n % 128:
        x = jnp.concatenate([x, jnp.zeros((-n % 128, 128), F32)], axis=0)
    return x.T[:, :n]


def staggered(make, widths):
    live, start = [], 0
    for width in widths:
        live.insert(0, make(start, width))
        start += width
        live = [x for x in live if advance(x)]
    while live:
        live = [x for x in live if advance(x)]


def ranges(widths):
    return [pl.ds(sum(widths[:k]), width) for k, width in enumerate(widths)]


def advance(x):
    try:
        next(x)
    except StopIteration:
        return False
    return True


def total(parts):
    return functools.reduce(jnp.add, parts)


def kernel(
    sizes,
    count_ref,
    pos_hbm,
    feat_hbm,
    face_hbm,
    edge_hbm,
    corner_hbm,
    centre_hbm,
    other_hbm,
    wpa_hbm,
    wpb_hbm,
    wr_hbm,
    w1_hbm,
    we_hbm,
    wv_hbm,
    w2_hbm,
    wout_ref,
    small_ref,
    fgrad_ref,
    pos_ref,
    feat_ref,
    face_ref,
    edge_ref,
    corner_ref,
    centre_ref,
    other_ref,
    wpa_ref,
    wpb_ref,
    wr_ref,
    w1_ref,
    we_ref,
    wv_ref,
    w2_ref,
    out_s,
    in_s,
    ret_s,
    oh_s,
    p_s,
    first_s,
    slope_s,
    q_s,
    v_s,
    ds2_s,
    dv_s,
    final_s,
    saved_s,
    acc_s,
    rows_s,
    bp_s,
    send_a,
    recv_a,
    send_b,
    recv_b,
    load,
):
    edges = centre_ref.shape[1]
    pairs = [
        (feat_hbm, feat_ref),
        (wpb_hbm, wpb_ref),
        (w1_hbm, w1_ref),
        (pos_hbm, pos_ref),
        (face_hbm, face_ref),
        (edge_hbm, edge_ref),
        (corner_hbm, corner_ref),
        (centre_hbm, centre_ref),
        (other_hbm, other_ref),
        (wpa_hbm, wpa_ref),
        (wr_hbm, wr_ref),
        (we_hbm, we_ref),
        (wv_hbm, wv_ref),
        (w2_hbm, w2_ref),
    ]
    loads = [pltpu.make_async_copy(src, dst, load.at[k]) for k, (src, dst) in enumerate(pairs)]
    for copy in loads[:7]:
        copy.start()
    greet(sizes)
    for copy in loads[7:]:
        copy.start()
    for copy in loads[:7]:
        copy.wait()

    feat = feat_ref[...]
    w1 = w1_ref[...]
    w1b = sum(dot(x, w1) for x in split(wpb_ref[...], 3))
    pb = dot32(feat, w1b)
    pos = jnp.concatenate([pos_ref[...], jnp.zeros((5, 128), F32)], axis=0)
    edge = jnp.concatenate([edge_ref[0].astype(F32), jnp.zeros((8, 116), F32)], axis=1)
    corner = jnp.concatenate([corner_ref[0].astype(F32), jnp.full((6, 8), -1.0, F32)], axis=0)
    corner = jnp.concatenate([corner, jnp.zeros((8, 120), F32)], axis=1)
    lists = jnp.concatenate([edge, corner, jnp.zeros((112, 128), F32)], axis=0).T.astype(jnp.int32)
    pieces = [face_ref[k] for k in range(6)] + [lists[k : k + 1, 0:8] for k in range(12)]
    pieces += [lists[k : k + 1, 8:16] for k in range(8)]
    slots = jnp.concatenate(pieces, axis=1)
    pick = (lax.broadcasted_iota(jnp.int32, (128, GHOSTS), 0) == slots).astype(F32).astype(BF16)
    out_s[:, 0:128] = dot(pick, pb.astype(BF16), TN)
    low = dot(jnp.concatenate([p.astype(F32) for p in split(pos, 3)], axis=0).astype(BF16), pick)
    out_s[:, 128:256] = lanes_to_rows(low[0:8] + low[8:16] + low[16:24], GHOSTS)
    greeted()
    ghosts = exchange(out_s, in_s, send_a, recv_a, 1, sizes)
    for copy in loads[7:]:
        copy.wait()

    iota = lax.broadcasted_iota(jnp.int32, (128, edges), 0).astype(F32).astype(BF16)
    one, zero = jnp.ones((), BF16), jnp.zeros((), BF16)
    cb = centre_ref[...].astype(F32).astype(BF16)
    o = other_ref[...]
    far = jnp.maximum(o - 416, 0)
    o = jnp.where(o < 416, o, 416 + (far >> 1) * 8 + (far & 1))
    oh_s[0:128, :] = jnp.where(iota == cb, one, zero)
    for t in range(4):
        n = 128 if t < 3 else 96
        ob = (o - 128 * t).astype(F32).astype(BF16)
        oh_s[128 * (t + 1) : 128 * (t + 1) + n, :] = jnp.where(iota[:n] == ob, one, zero)
    w1a = sum(dot(x, w1) for x in split(wpa_ref[...], 3))
    pa = dot32(feat, w1a)
    table = jnp.concatenate([pa.T, pb.T], axis=1).astype(BF16)
    both = jnp.concatenate([-pos, pos], axis=1)
    places = [p.astype(F32) for p in split(both, 3)]
    places = jnp.concatenate(places + [jnp.zeros_like(both)], axis=0).astype(BF16)
    p_s[...] = dot(jnp.concatenate([table, places], axis=0), oh_s[0:256, :])
    we = we_ref[...]
    wet = we.astype(F32).T.astype(BF16)
    wvt = wv_ref[...].astype(F32).T.astype(BF16)
    w2 = w2_ref[...]
    w2t = w2.astype(F32).T.astype(BF16)
    wback = jnp.concatenate([w2[:128], wv_ref[...]], axis=1)
    w2b = w2[128:]
    wr = sum(dot(x, w1) for x in split(jnp.concatenate([wr_ref[...], jnp.zeros((8, 128), F32)], axis=0), 3))[:8]
    wr_hi = wr.astype(BF16).astype(F32)
    wr_lo = wr - wr_hi
    wrt = jnp.concatenate([wr_hi, wr_lo, wr_hi, jnp.zeros((104, 128), F32)], axis=0).T[:, :32].astype(BF16)
    wr2 = jnp.concatenate([wr_hi, wr_lo], axis=0).astype(BF16)
    wout = jnp.broadcast_to(wout_ref[...].astype(F32), (128, 128)).T
    wout = jnp.concatenate([wout] * (edges // 128), axis=1)
    count = count_ref[0]

    ghosts.wait()
    got = in_s[...]
    gpos = rows_to_lanes(got[:, 128:])[:8]
    places = [p.astype(F32) for p in split(gpos, 3)]
    places = jnp.concatenate(places + [jnp.zeros_like(gpos)], axis=0).astype(BF16)
    table = jnp.concatenate([rows_to_lanes(got[:, :128]).astype(BF16), places], axis=0)

    def group(start, width):
        at = slice(start, start + width)
        cols = pl.ds(start, width)

        p = p_s[:, cols] + dot(table, oh_s[256:ROWS, cols])
        yield
        disp = p[128:136] + p[136:144] + p[144:152]
        dx, dy, dz = disp[0:1], disp[1:2], disp[2:3]
        sq = dx * dx + dy * dy + dz * dz + 0.01
        inv = lax.rsqrt(sq)
        dist = sq * inv
        ux, uy, uz = dx * inv, dy * inv, dz * inv
        is4 = 1.0 / (1.0 + 0.25 * dist * dist)
        g = is4 * is4
        gd = -dist * g * is4
        lane = lax.broadcasted_iota(jnp.int32, (1, width), 1) + start
        valid = jnp.where(lane < count, 1.0, 0.0)
        gv = g * valid
        h = g * inv
        hd = (gd - h) * inv
        order = lax.broadcasted_iota(jnp.int32, (8, width), 0).astype(F32) + 1.0
        sn, cs = sincos_turns(order * (0.25 * dist))
        basis = sn * h
        bp_s[:, cols] = order * (math.pi / 2) * cs * h + sn * hd
        rows_s[:, cols] = jnp.concatenate([ux, uy, uz, gv, inv, valid, gd, jnp.zeros_like(gd)], axis=0)
        b_hi = basis.astype(BF16).astype(F32)
        b4 = jnp.concatenate([b_hi, b_hi, basis - b_hi, jnp.zeros_like(basis)], axis=0).astype(BF16)
        z1 = p[:128] + dot(wrt, b4)
        yield
        sg = 0.5 * jnp.tanh(0.5 * z1) + 0.5
        f = z1 * sg
        first = f.astype(BF16)
        first_s[:, cols] = first
        slope_s[:, cols] = ((sg + f * (1.0 - sg)) * gv).astype(BF16)
        q = dot(wet, first)
        yield
        q_s[:, cols] = q.astype(BF16)
        mask = iota[:, at] == cb[:, at]
        pair = jnp.concatenate([q.astype(BF16), (q * uz).astype(BF16)], axis=0)
        env.append(dot(pair, moments(mask, gv, ux, uy, uz), NT))

    def group_b(start, width):
        at = slice(start, start + width)
        cols = pl.ds(start, width)
        rows = rows_s[:, cols]
        ux, uy, uz, gv = rows[0:1], rows[1:2], rows[2:3], rows[3:4]
        mask = iota[:, at] == cb[:, at]
        t4 = dot(left, select(mask, [jnp.ones_like(ux), ux, uy, uz]))
        yield
        tx, ty, tz = t4[128:256], t4[256:384], t4[384:512]
        t = t4[:128] + (0.5 * ux) * tx + (0.5 * uy) * ty + (0.5 * uz) * tz
        vf = v_s[:, cols].astype(F32)
        z2 = dot(w2t, jnp.concatenate([first_s[:, cols], (vf * t).astype(BF16)], axis=0))
        yield
        sg = 0.5 * jnp.tanh(0.5 * z2) + 0.5
        f = z2 * sg
        eo = jnp.sum(f.astype(BF16).astype(F32) * wout[:, at], axis=0, keepdims=True)
        ds2 = (wout[:, at] * (sg + f * (1.0 - sg))).astype(BF16)
        ds2_s[:, cols] = ds2
        dsc = dot(w2b, ds2)
        yield
        dv_s[:, cols] = (t * dsc).astype(BF16)
        y = vf * dsc
        du = [jnp.sum(y * c, axis=0, keepdims=True) for c in (tx, ty, tz)]
        saved_s[:, cols] = jnp.concatenate(du + [eo, jnp.zeros((4, width), F32)], axis=0)
        pair = jnp.concatenate([y.astype(BF16), (y * uz).astype(BF16)], axis=0)
        env.append(dot(pair, moments(mask, gv, ux, uy, uz), NT))

    def group_c(start, width):
        at = slice(start, start + width)
        cols = pl.ds(start, width)
        rows = rows_s[:, cols]
        ux, uy, uz, gv = rows[0:1], rows[1:2], rows[2:3], rows[3:4]
        mask = iota[:, at] == cb[:, at]
        d4 = dot(left, select(mask, [jnp.ones_like(ux), ux, uy, uz]))
        yield
        kx, ky, kz = d4[128:256], d4[256:384], d4[384:512]
        d = d4[:128] + (0.5 * ux) * kx + (0.5 * uy) * ky + (0.5 * uz) * kz
        qf = q_s[:, cols].astype(F32)
        saved = saved_s[:, cols]
        dux, duy, duz = [saved[j : j + 1] + jnp.sum(qf * c, axis=0, keepdims=True) for j, c in enumerate((kx, ky, kz))]
        dgq = jnp.sum(qf * d, axis=0, keepdims=True)
        df = p_s[0:128, cols] + dot(we, d.astype(BF16))
        yield
        dz1 = (df * slope_s[:, cols].astype(F32)).astype(BF16)
        db = dot(wr2, dz1)
        yield
        db = db[:8] + db[8:]
        inv, valid, gd = rows[4:5], rows[5:6], rows[6:7]
        dux, duy, duz = gv * dux, gv * duy, gv * duz
        eo = saved[3:4]
        dd = jnp.sum(db * bp_s[:, cols], axis=0, keepdims=True) + valid * (eo + dgq) * gd
        dd = dd - (dux * ux + duy * uy + duz * uz) * inv
        tail = [dux * inv + dd * ux, duy * inv + dd * uy, duz * inv + dd * uz, eo * gv, jnp.zeros((4, width), F32)]
        tail = jnp.concatenate(tail, axis=0)
        tail_hi = tail.astype(BF16).astype(F32)
        low = jnp.concatenate([tail_hi, tail - tail_hi], axis=0).astype(BF16)
        final = jnp.concatenate([dz1, low], axis=0)
        final_s[:, cols] = final
        env.append(dot(oh_s[256:ROWS, cols], final, NT))

    env = []
    staggered(group, WIDTHS)
    for cols in ranges(WIDTHS):
        v_s[:, cols] = dot(wvt, first_s[:, cols]).astype(BF16)
    left = left_operand(total(env), 0.2)
    env = []
    staggered(group_b, WIDTHS)
    for cols in ranges(WIDTHS):
        p_s[0:128, cols] = dot(wback, jnp.concatenate([ds2_s[:, cols], dv_s[:, cols]], axis=0))
    left = left_operand(total(env), 0.2)
    env = []
    staggered(group_c, WIDTHS)

    acc = total(env)
    out_s[:, 0:128] = acc[:, :128]
    out_s[:, 128:256] = jnp.concatenate([acc[:, 128:136] + acc[:, 136:144], jnp.zeros((GHOSTS, 120), F32)], axis=1)
    returns = exchange(out_s, ret_s, send_b, recv_b, -1, sizes)
    acc_s[...] = jnp.zeros_like(acc_s)

    def owned(k, carry):
        cols = pl.ds(pl.multiple_of(k * (edges // 2), 128), edges // 2)
        acc_s[...] += dot(oh_s[0:256, cols], final_s[:, cols], NT)
        return carry

    lax.fori_loop(0, 2, owned, 0)
    acc = acc_s[...]
    low = acc[:, 128:136] + acc[:, 136:144]
    low = jnp.concatenate([low, jnp.zeros((256, 120), F32)], axis=1).T[:8]
    part = dot32(acc[:128, :128], w1a, NT)
    own = acc[128:, :128]
    returns.wait()
    got = ret_s[...]
    a_hi, a_lo = split(got[:, :128], 2)
    own = own + (dot(pick, a_hi) + dot(pick, a_lo))
    back = [dot(pick, x) for x in split(got[:, 128:], 3)]
    back = (back[0] + back[1] + back[2]).T[:8]
    fgrad_ref[...] = part + dot32(own, w1b, NT)
    small_ref[...] = jnp.concatenate([low[0:3, :128] - low[0:3, 128:] - back[0:3], low[3:8, :128]], axis=0)


def place(small_ref, wide_ref, force_ref, energy_ref, fgrad_ref):
    force_ref[...] = small_ref[0:3, :]
    energy_ref[...] = small_ref[3:4, :]
    fgrad_ref[...] = wide_ref[...]


def local(
    sizes,
    positions,
    atom_features,
    send_face,
    send_edge,
    send_corner,
    centre,
    other,
    edge_count,
    w_proj_a,
    w_proj_b,
    w_radial,
    w_first,
    w_env,
    w_value,
    w_second,
    w_out,
):
    vm = pl.BlockSpec(memory_space=pltpu.VMEM)
    edges = centre.shape[0]
    operands = [
        positions,
        atom_features,
        jnp.transpose(send_face, (1, 0, 2)),
        jnp.transpose(send_edge, (0, 2, 1)),
        jnp.transpose(send_corner, (0, 2, 1)),
        centre.reshape(1, -1),
        other.reshape(1, -1),
        w_proj_a,
        w_proj_b,
        w_radial,
        w_first,
        w_env,
        w_value,
        w_second,
        w_out.reshape(1, -1),
    ]
    small, wide = pl.pallas_call(
        functools.partial(kernel, sizes),
        out_shape=[pltpu.VMEM((8, 128), F32), pltpu.VMEM((128, 128), F32)],
        in_specs=[pl.BlockSpec(memory_space=pltpu.SMEM)] + [pl.BlockSpec(memory_space=pl.ANY)] * 14 + [vm],
        out_specs=[vm] * 2,
        scratch_shapes=[pltpu.VMEM(x.shape, x.dtype) for x in operands[:14]]
        + [
            pltpu.VMEM((GHOSTS, 256), F32),
            pltpu.VMEM((GHOSTS, 256), F32),
            pltpu.VMEM((GHOSTS, 256), F32),
            pltpu.VMEM((ROWS, edges), BF16),
            pltpu.VMEM((160, edges), F32),
            *[pltpu.VMEM((128, edges), BF16)] * 6,
            pltpu.VMEM((144, edges), BF16),
            pltpu.VMEM((8, edges), F32),
            pltpu.VMEM((256, 144), F32),
            pltpu.VMEM((8, edges), F32),
            pltpu.VMEM((8, edges), F32),
        ]
        + [pltpu.SemaphoreType.DMA(())] * 4
        + [pltpu.SemaphoreType.DMA((14,))],
        compiler_params=pltpu.CompilerParams(
            collective_id=0, has_side_effects=True, vmem_limit_bytes=56 * 2**20
        ),
    )(edge_count, *operands)
    force, energy, fgrad = pl.pallas_call(
        place,
        out_shape=[
            jax.ShapeDtypeStruct((3, 128), F32),
            jax.ShapeDtypeStruct((1, 128), F32),
            jax.ShapeDtypeStruct((128, 128), F32),
        ],
        in_specs=[vm] * 2,
        out_specs=[vm] * 3,
    )(*[pltpu.with_memory_space_constraint(x, pltpu.VMEM) for x in (small, wide)])
    return force, energy.reshape(-1), fgrad


def solution(mesh):
    axes = ("gx", "gy", "gz")
    sizes = tuple(mesh.shape[a] for a in axes)
    split_first = [P(axes, None), P(axes, None, None), P(axes, None, None), P(axes, None, None)]
    return jax.shard_map(
        functools.partial(local, sizes),
        mesh=mesh,
        in_specs=(P(None, axes), *split_first, P(axes), P(axes), P(axes)) + (P(),) * 8,
        out_specs=(P(None, axes), P(axes), P(axes, None)),
        check_vma=False,
    )
```
